32 devices in a mesh: req: 8 (over z, x), kv: 4 (over y, core).
Axes of the slice: x: 2, y: 2, z: 4, core: 2. Of those that a mesh axis runs over, the one named last changes fastest.
Arguments:
- hidden_in: bfloat16 [1024, 1536], P('req'), may hold values from -6 to 6
- attn_gain: float32 [1536], replicated, may hold values from 0.1 to 1.9
- w_query: bfloat16 [1536, 1536], P('kv'), may hold values from -0.15625 to 0.15625
- w_key: bfloat16 [512, 1536], P('kv'), may hold values from -0.15625 to 0.15625
- w_value: bfloat16 [512, 1536], P('kv'), may hold values from -0.15625 to 0.15625
- w_out: bfloat16 [1536, 1536], P('kv'), may hold values from -0.75 to 0.75
- k_cache: bfloat16 [3072, 8, 8192], P('req', 'kv'), may hold values from -600 to 600
- v_cache: bfloat16 [3072, 8, 8192], P('req', 'kv'), may hold values from -6 to 6
- cache_len: int32 [1024], replicated, may hold values from 1 to 384, 196608 in all
- block_slot: int32 [3072], P('req'), may hold values from 0 to 3071, as said below
- moe_gain: float32 [1536], replicated, may hold values from 0.1 to 1.9
- w_router: bfloat16 [1536, 16], replicated, may hold values from -0.15625 to 0.15625
- w_gate_up: bfloat16 [16, 1536, 1024], P('req'), may hold values from -0.15625 to 0.15625
- w_down: bfloat16 [16, 512, 1536], P('req'), may hold values from -0.25 to 0.25
- routes: int32 [1024, 8], P(('req', 'kv')), may hold values from 0 to 15, all different within a row; in each aligned block of 32 rows (0 to 31, 32 to 63, ...) at most 32 rows name the same one
Outputs:
- layer_out: bfloat16 [1024, 1536], P(('req', 'kv'))
The draws below stay inside these ranges and needn't reach their ends.
Inputs may be any that keep to these rules, and one draw needn't show every extreme that they name: `block_slot`: each value once; the block holds page v % 3 of request v // 3; the blocks of one index of req hold exactly 128 * 3 / 8 pages of the requests of each index of req. `routes`: each row names 8 different experts; in the 32 rows of one device an expert may be named by all of them.
All inputs are finite; a program needn't handle non-finite values.
Results may differ from the reference program's by a relative error of at most 0.02.
The reference program's roundings to bfloat16 on the way (of `normed`, `query`, `key_new`, `value_new`, `attended`, `moe_in`, `activated` and `expert_out`) count: a program that leaves them out, or rounds other values in their place, can miss the bound.
Values may be sent and summed in bfloat16 or wider, within the bound.
No kernel may reach another device: no remote copies, remote signals or barrier semaphores. Data moves between devices by JAX's collectives and lax.ppermute only.
A program may use at most 192 MiB of HBM per device.

```python
import math
import jax
import jax.numpy as jnp
import numpy as np
from jax import lax

D = 1536
HEADS = 24
KVH = 8
HD = 64
FFE = 512
TOPK = 8
R_DEV = 128
MAXLEN = 384
BLK = 128
PAGES = 3
REQUESTS = 1024
NBLOCKS = 3072
TOK_DEV = 32
EXPERTS = 16
N_REQ = 8


def draw_k_cache(key, part):
    first = jax.random.fold_in(key, 0)
    base = jnp.clip(jax.random.normal(first, (NBLOCKS, KVH, BLK, HD), jnp.float32), -4.0, 4.0)
    return base.reshape(NBLOCKS, KVH, BLK * HD).astype(jnp.bfloat16)


def draw_block_slot(key, part):
    per_home = R_DEV * PAGES
    share = per_home // N_REQ
    first, second = jax.random.split(jax.random.fold_in(key, 17))
    home_keys = jax.random.split(first, N_REQ)
    home_perms = jax.vmap(lambda k: jax.random.permutation(k, per_home))(home_keys).astype(jnp.int32)
    device_ids = jnp.arange(N_REQ, dtype=jnp.int32)[:, None]
    slot_ids = jnp.arange(per_home, dtype=jnp.int32)[None, :]
    home_ids = slot_ids // share
    picked = home_perms[home_ids, device_ids * share + slot_ids % share]
    values = (home_ids * per_home + picked).astype(jnp.int32)
    shuffle_keys = jax.random.split(second, N_REQ)
    shuffles = jax.vmap(lambda k: jax.random.permutation(k, per_home))(shuffle_keys).astype(jnp.int32)
    values = jnp.take_along_axis(values, shuffles, 1)
    return values.reshape(-1).astype(jnp.int32)


def levels(rng, shape, shards, least, largest):
    def one(position, shards_of):
        steps = jax.random.uniform(jax.random.fold_in(jax.random.fold_in(rng, 6), position), (shards_of,), jnp.float32, least / len(shards), largest / len(shards))
        return jnp.repeat(jnp.exp(steps), shape[position] // shards_of).reshape((-1,) + (1,) * (len(shape) - position - 1))

    level = one(*shards[0])
    for cut in shards[1:]:
        level = level * one(*cut)
    return level


def split_up(number_of, total, bound, lean):
    weights = [(1 << 20) // math.isqrt(rank ** lean) + 1 for rank in range(2, number_of + 1)]
    rest, holding = total - bound - (number_of - 1), [1] * (number_of - 1)
    while rest > 0:
        free = [i for i in range(number_of - 1) if holding[i] < bound]
        mass, left = sum([weights[i] for i in free]), rest
        for i in free:
            addition = min(bound - holding[i], max(1, left * weights[i] // mass), rest)
            holding[i] = holding[i] + addition
            rest = rest - addition
    return np.array([bound] + holding)


def uneven(stream_key, amount, total, bound, lean):
    if amount == 2:
        one = jax.random.randint(stream_key, (), max(1, total - bound), min(bound, total - 1) + 1)
        return jnp.stack([one, total - one])
    lengths = jnp.asarray(split_up(amount, total, bound, lean), jnp.int32)
    couples = (amount - 1) // 2
    giver, receiver = lengths[1:1 + 2 * couples:2], lengths[2:2 + 2 * couples:2]
    room = jnp.minimum(giver - 1, bound - receiver)
    passed = jax.random.randint(jax.random.fold_in(stream_key, 1), (couples,), 0, 1 << 20) % (room + 1)
    lengths = lengths.at[1:1 + 2 * couples:2].set(giver - passed).at[2:2 + 2 * couples:2].set(receiver + passed)
    return lengths[jax.random.permutation(jax.random.fold_in(stream_key, 2), amount)]


def routed_block(key, own, number, rows, count, top, limit, lean):
    sequence = jax.random.permutation(key, count)
    heavy_load, usual = portions_of(count, rows * top, limit, lean, True), portions_of(count, rows * top, limit, lean, False)
    places = jnp.arange(count)

    def named(tallies, turn):
        used = int((tallies > 0).sum())
        fixed = max(1, used // 4)
        moved = fixed + (places - fixed + turn * (used - fixed)) % max(1, count - fixed)
        return jnp.zeros((count,), jnp.int32).at[sequence[jnp.where(places < fixed, places, moved)]].set(jnp.asarray(tallies, jnp.int32))

    tallies = jnp.where(number % 4 == 0, named(heavy_load, number // 4), named(usual, number - number // 4 - 1))
    mixed = jax.random.permutation(jax.random.fold_in(own, 3), count)
    donor, taker = mixed[0:count // 2 * 2:2], mixed[1:count // 2 * 2:2]
    margin = jnp.minimum(tallies[donor] - 1, limit - tallies[taker]) // 2
    margin = jnp.where((donor == sequence[0]) | (taker == sequence[0]) | (tallies[taker] == 0), 0, jnp.maximum(margin, 0))
    moved = jax.random.randint(jax.random.fold_in(own, 4), (count // 2,), 0, 1 << 20) % (margin + 1)
    tallies = tallies.at[donor].add(-moved).at[taker].add(moved)
    labels = jnp.searchsorted(jnp.cumsum(tallies), jnp.arange(rows * top), side="right").astype(jnp.int32)
    table = labels.reshape(top, rows).T
    table = table[jax.random.permutation(jax.random.fold_in(own, 1), rows)]
    turn = jax.random.randint(jax.random.fold_in(own, 2), (rows, 1), 0, top)
    return jnp.take_along_axis(table, (jnp.arange(top)[None, :] + turn) % top, axis=1)


def portions_of(number_of, total, limit, lean, full):
    weights = [(1 << 20) // math.isqrt(standing ** lean) + 1 for standing in range(1, number_of + 1)]
    largest = limit if full else min(limit, max(-(-total // number_of), total * weights[0] // sum(weights)))
    least = 1 if total - largest >= number_of - 1 else 0
    counts, rest = [largest] + [least] * (number_of - 1), total - largest - least * (number_of - 1)
    while rest > 0:
        movable = [i for i in range(1, number_of) if counts[i] < largest] or [i for i in range(1, number_of) if counts[i] < limit]
        whole, budget = sum([weights[i] for i in movable]), rest
        for i in movable:
            extra = min(limit - counts[i], max(1, budget * weights[i] // whole), rest)
            counts[i] = counts[i] + extra
            rest = rest - extra
    return np.array(counts)


def gaussian(rng, dims, width, limit, shards=(), kind=jnp.bfloat16):
    level = levels(rng, dims, shards, -0.22, 0.18) if shards else 1.0
    drawn = jax.random.normal(rng, dims, jnp.float32) * width * level
    return jnp.minimum(jnp.maximum(drawn, -limit), limit).astype(kind)


def setup_inputs(seed: int = 0) -> dict:
    splits = jax.random.split(jax.random.key(seed), 16)
    hidden_in = gaussian(splits[0], (REQUESTS, D), 1.0, 6.0, ((0, 8),))
    attn_gain = jnp.clip(1.0 + 0.18 * jax.random.normal(splits[1], (D,), jnp.float32), 0.1, 1.9)
    w_query = gaussian(splits[2], (HEADS * HD, D), D ** -0.5, 0.15625, ((0, 4),))
    w_key = gaussian(splits[3], (KVH * HD, D), D ** -0.5, 0.15625, ((0, 4),))
    w_value = gaussian(splits[4], (KVH * HD, D), D ** -0.5, 0.15625, ((0, 4),))
    w_out = gaussian(splits[5], (HEADS * HD, D), HD ** -0.5, 0.75, ((0, 4),))
    k_cache = draw_k_cache(jax.random.fold_in(splits[15], 71), 0)
    v_cache = gaussian(splits[7], (NBLOCKS, KVH, BLK * HD), 1.0, 6.0, ((0, 8), (1, 4)))
    cache_len = uneven(splits[8], REQUESTS, REQUESTS * MAXLEN // 2, MAXLEN, 2).astype(jnp.int32)
    block_slot = draw_block_slot(jax.random.fold_in(splits[15], 71), 0)
    moe_gain = jnp.clip(1.0 + 0.18 * jax.random.normal(splits[10], (D,), jnp.float32), 0.1, 1.9)
    w_router = gaussian(splits[11], (D, EXPERTS), D ** -0.5, 0.15625)
    w_gate_up = gaussian(splits[12], (EXPERTS, D, 2 * FFE), D ** -0.5, 0.15625, ((0, 8),))
    w_down = gaussian(splits[13], (EXPERTS, FFE, D), FFE ** -0.5, 0.25, ((0, 8),))
    routes_keys = jax.random.split(jax.random.fold_in(splits[14], 1), REQUESTS // TOK_DEV)
    routes_turns = jax.random.permutation(jax.random.fold_in(splits[14], 3), REQUESTS // TOK_DEV)
    routes = jax.vmap(lambda own, number: routed_block(jax.random.fold_in(splits[14], 2), own, number, TOK_DEV, EXPERTS, TOPK, TOK_DEV, 2))(routes_keys, routes_turns).reshape((REQUESTS, TOPK))
    return {"hidden_in": hidden_in, "attn_gain": attn_gain, "w_query": w_query, "w_key": w_key, "w_value": w_value, "w_out": w_out, "k_cache": k_cache, "v_cache": v_cache, "cache_len": cache_len, "block_slot": block_slot, "moe_gain": moe_gain, "w_router": w_router, "w_gate_up": w_gate_up, "w_down": w_down, "routes": routes}


def rms_norm(values, gain):
    values = values.astype(jnp.float32)
    return values * lax.rsqrt(lax.optimization_barrier(jnp.mean(values * values, -1, keepdims=True)) + 1e-05) * gain

def rotate(values, positions):
    half_dim = values.shape[-1] // 2
    frequency = 10000.0 ** (-jnp.arange(half_dim, dtype=jnp.float32) / half_dim)
    angles = positions.astype(jnp.float32)[:, None, None] * frequency
    cosines = jnp.cos(angles)
    sines = jnp.sin(angles)
    first_half = values[..., :half_dim]
    second_half = values[..., half_dim:]
    return jnp.concatenate([first_half * cosines - second_half * sines, first_half * sines + second_half * cosines], -1)

def project_rows(normed, weight):
    return lax.dot_general(normed, weight, (((1,), (1,)), ((), ())), preferred_element_type=jnp.float32)

def by_position(blocks_data):
    return blocks_data.reshape(R_DEV, PAGES, KVH, BLK, HD).transpose(0, 1, 3, 2, 4).reshape(R_DEV, MAXLEN, KVH, HD)

def reference(hidden_in, attn_gain, w_query, w_key, w_value, w_out, k_cache, v_cache, cache_len, block_slot, moe_gain, w_router, w_gate_up, w_down, routes):
    request_count = hidden_in.shape[0]
    normed = rms_norm(hidden_in, attn_gain).astype(jnp.bfloat16)
    query = project_rows(normed, w_query).reshape(request_count, HEADS, HD)
    query = (rotate(query, cache_len) * 0.125).astype(jnp.bfloat16)
    key_new = project_rows(normed, w_key).reshape(request_count, KVH, HD)
    key_new = rotate(key_new, cache_len).astype(jnp.bfloat16)
    value_new = project_rows(normed, w_value).astype(jnp.bfloat16).reshape(request_count, KVH, HD)
    block_of_slot = jnp.argsort(block_slot).astype(jnp.int32)
    positions = jnp.arange(MAXLEN, dtype=jnp.int32)
    per_group = HEADS // KVH

    def attend(group_index):
        request_rows = group_index * R_DEV + jnp.arange(R_DEV, dtype=jnp.int32)
        slot_ids = request_rows[:, None] * PAGES + jnp.arange(PAGES, dtype=jnp.int32)[None, :]
        blocks = block_of_slot[slot_ids.reshape(-1)]
        cache_keys = by_position(k_cache[blocks]).astype(jnp.float32)
        cache_values = by_position(v_cache[blocks]).astype(jnp.float32)
        start = (group_index * R_DEV).astype(jnp.int32)
        query_group = lax.dynamic_slice_in_dim(query, start, R_DEV, 0).reshape(R_DEV, KVH, per_group, HD).astype(jnp.float32)
        newkey_group = lax.dynamic_slice_in_dim(key_new, start, R_DEV, 0).astype(jnp.float32)
        newvalue_group = lax.dynamic_slice_in_dim(value_new, start, R_DEV, 0).astype(jnp.float32)
        length_group = lax.dynamic_slice_in_dim(cache_len, start, R_DEV, 0)
        scores = jnp.einsum('rgqd,rtgd->rgqt', query_group, cache_keys, precision=lax.Precision.HIGHEST)
        usable = positions[None, :] < length_group[:, None]
        scores = jnp.where(usable[:, None, None, :], scores, -jnp.inf)
        own_score = jnp.einsum('rgqd,rgd->rgq', query_group, newkey_group, precision=lax.Precision.HIGHEST)
        highest = jnp.maximum(lax.optimization_barrier(jnp.max(scores, -1)), own_score)
        weights = jnp.exp(scores - highest[..., None])
        own_weight = jnp.exp(own_score - highest)
        total = lax.optimization_barrier(jnp.sum(weights, -1)) + own_weight
        numer = jnp.einsum('rgqt,rtgd->rgqd', weights, cache_values, precision=lax.Precision.HIGHEST)
        numer = numer + own_weight[..., None] * newvalue_group[:, :, None, :]
        return (numer / total[..., None]).reshape(R_DEV, HEADS * HD)
    attended = lax.map(attend, jnp.arange(N_REQ, dtype=jnp.int32)).reshape(request_count, HEADS * HD).astype(jnp.bfloat16)
    after_attn = hidden_in.astype(jnp.float32) + jnp.dot(attended, w_out, preferred_element_type=jnp.float32)
    moe_in = rms_norm(after_attn, moe_gain).astype(jnp.bfloat16)
    logits = jnp.dot(moe_in, w_router, preferred_element_type=jnp.float32)
    chosen = jnp.take_along_axis(logits, routes, 1)
    gate_probs = jax.nn.softmax(chosen, -1)
    flat_expert = routes.reshape(-1)
    order = jnp.argsort(flat_expert).astype(jnp.int32)
    token_of = (order // TOPK).astype(jnp.int32)
    expert_count = w_router.shape[1]
    group_sizes = lax.optimization_barrier(jnp.sum((flat_expert[:, None] == jnp.arange(expert_count, dtype=jnp.int32)[None, :]).astype(jnp.int32), 0)).astype(jnp.int32)
    expert_in = moe_in[token_of]
    gate_up = lax.ragged_dot(expert_in, w_gate_up, group_sizes, preferred_element_type=jnp.float32)
    activated = (jax.nn.silu(gate_up[:, :FFE]) * gate_up[:, FFE:]).astype(jnp.bfloat16)
    expert_out = lax.ragged_dot(activated, w_down, group_sizes, preferred_element_type=jnp.float32).astype(jnp.bfloat16)
    weight = gate_probs.reshape(-1)[order]
    mixture = jax.ops.segment_sum(expert_out.astype(jnp.float32) * weight[:, None], token_of, num_segments=request_count)
    return (after_attn + mixture).astype(jnp.bfloat16)
```

```python
import functools

import jax
import jax.numpy as jnp
from jax import lax
from jax.experimental import pallas as pl
from jax.experimental.pallas import tpu as pltpu
from jax.sharding import PartitionSpec as P

HD = 64
FFE = 512
BLK = 128
PAGES = 3
NEG = -1e30
BF = jnp.bfloat16
F32 = jnp.float32


def iota(shape, dim):
    return lax.broadcasted_iota(jnp.int32, shape, dim)


def swap(value, axis, distance):
    size = lax.axis_size(axis)
    return lax.ppermute(value, axis, [(source, source ^ distance) for source in range(size)])


def rms_norm(values, gain):
    values = values.astype(F32)
    return values * lax.rsqrt(jnp.mean(values * values, -1, keepdims=True) + 1e-05) * gain


def rotate(values, positions):
    half_dim = values.shape[-1] // 2
    frequency = 10000.0 ** (-jnp.arange(half_dim, dtype=F32) / half_dim)
    angles = positions.astype(F32)[:, None, None] * frequency
    cosines = jnp.cos(angles)
    sines = jnp.sin(angles)
    first_half = values[..., :half_dim]
    second_half = values[..., half_dim:]
    return jnp.concatenate(
        [first_half * cosines - second_half * sines, first_half * sines + second_half * cosines], -1
    )


def project_rows(normed, weight):
    return lax.dot_general(normed, weight, (((1,), (1,)), ((), ())), preferred_element_type=F32)


def dot(left, right):
    return jnp.dot(left, right, preferred_element_type=F32)


def attend_kernel(heads, groups, chunk, qrow_ref, left_ref, slot_ref, local_ref, query_ref,
                  key_ref, value_ref, out_ref, rows_ref):
    blocks = key_ref.shape[0]
    lanes = key_ref.shape[1]
    width = out_ref.shape[1]
    per_group = heads // groups
    feature = heads * HD

    row = iota((chunk * 16, 1), 0)
    parity = (row // 8) % 2
    head = row % 8
    keep_head = iota((chunk * 16, feature), 1) // HD == head
    keep_half = iota((chunk * 16, 2 * HD), 1) // HD == parity
    fold = (iota((feature, 2 * HD), 0) % HD == iota((feature, 2 * HD), 1) % HD).astype(BF)
    spread = (iota((chunk * 16, chunk), 0) // 16 == iota((chunk * 16, chunk), 1)).astype(BF)
    gather = (iota((chunk, chunk * 8), 1) // 8 == iota((chunk, chunk * 8), 0)).astype(BF)
    cell_row = iota((16, lanes), 0)
    cell_lane = iota((16, lanes), 1)
    position = jnp.where(
        cell_lane % groups == (cell_row % 8) // per_group,
        2 * (cell_lane // groups) + cell_row // 8,
        1 << 20,
    )[None]
    out_head = iota((chunk * 8, 1), 0) % 8
    out_lane = iota((chunk * 8, width), 1)
    own_lanes = out_lane // HD == out_head
    extra = out_lane - feature
    part_at = [jnp.logical_and(extra == out_head * 4 + part, out_head < heads) for part in range(3)]

    def step(index, carry):
        base = pl.multiple_of(index * chunk, chunk)
        rows = pl.ds(base, chunk)
        picked = (iota((chunk, query_ref.shape[0]), 1) == qrow_ref[rows, :]).astype(BF)
        query = dot(picked, query_ref[...]).astype(BF)
        query = jnp.where(keep_head, dot(spread, query), 0.0).astype(BF)
        query = jnp.where(keep_half, dot(query, fold), 0.0).astype(BF).reshape(chunk, 16, 2 * HD)
        scores = lax.dot_general(
            query, key_ref[rows], (((2,), (2,)), ((0,), (0,))), preferred_element_type=F32
        )
        usable = position < left_ref[rows]
        scores = jnp.where(usable, scores, NEG)
        highest = jnp.max(scores, -1, keepdims=True)
        highest = jnp.maximum(highest[:, :8], highest[:, 8:])
        weights = jnp.where(usable, jnp.exp(scores - jnp.concatenate([highest, highest], 1)), 0.0)
        total = jnp.sum(weights, -1, keepdims=True)
        total = total[:, :8] + total[:, 8:]
        numer = lax.dot_general(
            weights.astype(BF), value_ref[rows], (((2,), (1,)), ((0,), (0,))), preferred_element_type=F32
        )
        numer = jnp.where(iota((1, 8, 2 * HD), 2) < HD, numer[:, :8], numer[:, 8:])
        numer = numer.reshape(chunk * 8, 2 * HD)
        numer = numer + pltpu.roll(numer, HD, 1)
        total = total.reshape(chunk * 8, 1)
        highest = highest.reshape(chunk * 8, 1)
        some = total > 0.0
        safe = jnp.where(some, total, 1.0)
        mean = numer / safe
        level = jnp.where(some, highest + jnp.log(safe), NEG)
        first = level.astype(BF).astype(F32)
        second = (level - first).astype(BF).astype(F32)
        third = level - first - second
        wide = jnp.concatenate([mean] * (width // (2 * HD)), 1)
        wide = jnp.where(own_lanes, wide, 0.0)
        for here, part in zip(part_at, (first, second, third)):
            wide = jnp.where(here, part, wide)
        packed = dot(gather, wide.astype(BF))
        lane = iota((chunk, width), 1)
        packed = jnp.where(lane == feature + HD - 1, local_ref[rows, :].astype(F32), packed)
        rows_ref[rows, :] = packed.astype(BF)
        return carry

    lax.fori_loop(0, blocks // chunk, step, 0)
    order = (slot_ref[...] == iota((blocks, blocks), 0)).astype(BF)
    out_ref[...] = dot(order, rows_ref[...]).astype(BF)


def merge_kernel(heads, groups, part_ref, query_ref, key_ref, value_ref, weight_ref, out_ref):
    rows = query_ref.shape[0]
    blocks, width = part_ref.shape
    per_group = heads // groups
    feature = heads * HD
    row = iota((32, width), 0)
    column = iota((32, width), 1) - feature
    wanted = jnp.where(row < 24, (row % 8) * 4 + row // 8, HD - 1)
    pick = jnp.logical_and(column == wanted, jnp.logical_or(row == 24, row % 8 < heads))
    pick = jnp.logical_and(pick, row <= 24).astype(BF)
    parts = part_ref[...]
    extras = lax.dot_general(pick, parts, (((1,), (1,)), ((), ())), preferred_element_type=F32)
    levels = extras[0:8] + extras[8:16] + extras[16:24]
    local = extras[24:25].astype(jnp.int32)
    member = local == iota((rows, blocks), 0)

    source = iota((groups * HD, width), 0)
    target = iota((groups * HD, width), 1)
    same = jnp.logical_and(source // HD == target // (HD * per_group), source % HD == target % HD)
    widen = same.astype(BF)
    key = dot(key_ref[...], widen)
    value = dot(value_ref[...], widen)
    products = query_ref[...].astype(F32) * key[:, :feature]
    lane_head = iota((rows, width), 1) // HD
    joined = jnp.zeros((rows, width), F32)
    for head in range(heads):
        own = jnp.sum(jnp.where(lane_head[:, :feature] == head, products, 0.0), -1, keepdims=True)
        level = levels[head : head + 1]
        highest = jnp.max(jnp.where(member, level, NEG), -1, keepdims=True)
        highest = jnp.maximum(highest, own)
        weights = jnp.where(member, jnp.exp(level - highest), 0.0).astype(BF)
        own_weight = jnp.exp(own - highest)
        total = jnp.sum(weights.astype(F32), -1, keepdims=True) + own_weight
        numer = dot(weights, parts) + own_weight * value
        joined = jnp.where(lane_head == head, numer / total, joined)
    attended = joined[:, :feature].astype(BF)
    out_ref[...] = dot(attended, weight_ref[...]).astype(BF)


def shards(
    hidden_in,
    attn_gain,
    w_query,
    w_key,
    w_value,
    w_out,
    k_cache,
    v_cache,
    cache_len,
    block_slot,
    moe_gain,
    w_router,
    w_gate_up,
    w_down,
    routes,
):
    req_index = lax.axis_index("req")
    kv_index = lax.axis_index("kv")
    sources = lax.axis_size("req")
    kv_size = lax.axis_size("kv")
    row_count, model = hidden_in.shape
    heads = w_query.shape[0] // HD
    groups = w_key.shape[0] // HD
    blocks = k_cache.shape[0]
    requests = cache_len.shape[0]
    share = blocks // sources
    width = -(-(heads * HD + HD) // 128) * 128

    lengths_home = lax.dynamic_slice_in_dim(cache_len, req_index * row_count, row_count, 0)
    normed = rms_norm(hidden_in, attn_gain).astype(BF)
    query = project_rows(normed, w_query).reshape(row_count, heads, HD)
    query = (rotate(query, lengths_home) * 0.125).astype(BF).reshape(row_count, heads * HD)
    key_new = project_rows(normed, w_key).reshape(row_count, groups, HD)
    key_new = rotate(key_new, lengths_home).astype(BF).reshape(row_count, groups * HD)
    value_new = project_rows(normed, w_value).astype(BF)
    queries = jnp.concatenate(
        [query] + [swap(query, "req", distance) for distance in range(1, sources)], 0
    )

    owners = block_slot // PAGES
    home = owners // row_count
    local = owners % row_count
    owned = owners[:, None] == jnp.arange(requests, dtype=jnp.int32)[None, :]
    lengths = jnp.sum(jnp.where(owned, cache_len[None, :], 0), 1)
    left = lengths - (block_slot % PAGES) * BLK
    left = jnp.broadcast_to(left[:, None, None], (blocks, 1, groups * HD))
    number = jnp.arange(blocks, dtype=jnp.int32)
    earlier = jnp.logical_and(home[:, None] == home[None, :], number[:, None] < number[None, :])
    rank = jnp.sum(earlier.astype(jnp.int32), 0)
    slot = home * share + rank
    query_row = jnp.bitwise_xor(home, req_index) * row_count + local

    def pairs(cache):
        cache = cache.reshape(blocks, groups, HD, 2 * HD).transpose(0, 2, 1, 3)
        return cache.reshape(blocks, HD * groups, 2 * HD)

    chunk = 48
    vmem = pl.BlockSpec(memory_space=pltpu.VMEM)
    partial = pl.pallas_call(
        functools.partial(attend_kernel, heads, groups, chunk),
        out_shape=jax.ShapeDtypeStruct((blocks, width), BF),
        in_specs=[vmem] * 7,
        out_specs=vmem,
        scratch_shapes=[pltpu.VMEM((blocks, width), BF)],
        compiler_params=pltpu.CompilerParams(vmem_limit_bytes=48 << 20),
        name="attend",
    )(
        query_row[:, None],
        left,
        slot[None, :],
        local[:, None],
        queries,
        pairs(k_cache),
        pairs(v_cache),
    )
    parts = lax.all_to_all(partial, "req", split_axis=0, concat_axis=0, tiled=True)
    projected = pl.pallas_call(
        functools.partial(merge_kernel, heads, groups),
        out_shape=jax.ShapeDtypeStruct((row_count, model), BF),
        in_specs=[vmem] * 5,
        out_specs=vmem,
        compiler_params=pltpu.CompilerParams(vmem_limit_bytes=32 << 20),
        name="merge",
    )(parts, query, key_new, value_new, w_out)

    token_count = row_count // kv_size
    attn_rows = jnp.zeros((token_count, model), F32)
    for distance in range(kv_size):
        start = jnp.bitwise_xor(kv_index, distance) * token_count
        piece = lax.dynamic_slice_in_dim(projected, start, token_count, 0)
        if distance:
            piece = swap(piece, "kv", distance)
        attn_rows = attn_rows + piece.astype(F32)
    rows_home = lax.dynamic_slice_in_dim(hidden_in, kv_index * token_count, token_count, 0)
    after_attn = rows_home.astype(F32) + attn_rows
    moe_in = rms_norm(after_attn, moe_gain).astype(BF)
    logits = dot(moe_in, w_router)
    experts = w_router.shape[1]
    named = routes[:, :, None] == jnp.arange(experts, dtype=jnp.int32)[None, None, :]
    chosen = jnp.any(named, 1)
    gates = jax.nn.softmax(jnp.where(chosen, logits, -jnp.inf), -1)
    gates_high = gates.astype(BF)
    gates_low = (gates - gates_high.astype(F32)).astype(BF)
    outgoing = jnp.concatenate(
        [moe_in, gates_high, gates_low, jnp.zeros((token_count, 128 - 2 * experts), BF)], 1
    )
    arrived = jnp.concatenate(
        [outgoing] + [swap(outgoing, "req", distance) for distance in range(1, sources)], 0
    )
    tokens = arrived[:, :model]
    local_experts = w_gate_up.shape[0]
    first = model + req_index * local_experts
    high = lax.dynamic_slice_in_dim(arrived, first, local_experts, 1).astype(F32)
    low = lax.dynamic_slice_in_dim(arrived, first + experts, local_experts, 1).astype(F32)
    gate_here = high + low
    gate_up = jnp.einsum("td,edf->etf", tokens, w_gate_up, preferred_element_type=F32)
    activated = (jax.nn.silu(gate_up[..., :FFE]) * gate_up[..., FFE:]).astype(BF)
    produced = jnp.einsum("etf,efd->etd", activated, w_down, preferred_element_type=F32)
    produced = produced.astype(BF).astype(F32)
    mixed = jnp.sum(produced * gate_here.T[:, :, None], 0).astype(BF)
    mixture = mixed[:token_count].astype(F32)
    for distance in range(1, sources):
        piece = mixed[distance * token_count : (distance + 1) * token_count]
        mixture = mixture + swap(piece, "req", distance).astype(F32)
    return (after_attn + mixture).astype(BF)


def solution(mesh):
    placed = (
        P("req", None),
        P(),
        P("kv", None),
        P("kv", None),
        P("kv", None),
        P("kv", None),
        P("req", "kv", None),
        P("req", "kv", None),
        P(),
        P("req"),
        P(),
        P(),
        P("req", None, None),
        P("req", None, None),
        P(("req", "kv"), None),
    )
    return jax.shard_map(
        shards, mesh=mesh, in_specs=placed, out_specs=P(("req", "kv"), None), check_vma=False
    )
```

```python
import functools

import jax
import jax.numpy as jnp
import numpy as np
from jax import lax
from jax.experimental import pallas as pl
from jax.experimental.pallas import tpu as pltpu
from jax.sharding import PartitionSpec as P

HD = 64
FFE = 512
BLK = 128
PAGES = 3
CHUNK = 96
COSTS = (12.0, 3.0, 12.0, 12.0, 12.0, 4.0, 12.0)
NEG = -1e30
BF = jnp.bfloat16
F32 = jnp.float32


def iota(shape, dim):
    return lax.broadcasted_iota(jnp.int32, shape, dim)


def swap(value, axis, distance):
    size = lax.axis_size(axis)
    return lax.ppermute(value, axis, [(source, source ^ distance) for source in range(size)])


def gather_rows(value, axis):
    size = lax.axis_size(axis)
    held = {0: value}
    far = size // 2
    for distance in list(range(far, size, 2)) + list(range(2, far, 2)) + list(range(1, far, 2)):
        held[distance] = swap(value, axis, distance)
    for distance in range(far + 1, size, 2):
        held[distance] = swap(held[distance - 1], axis, 1)
    return [held[distance] for distance in range(size)]


def send_rows(values, axis):
    size = lax.axis_size(axis)
    held = {0: values[0]}
    far = size // 2
    for start in list(range(size - 2, far - 1, -2)) + list(range(2, far, 2)) + [0]:
        for distance in (start, start + 1):
            if distance:
                held[distance] = swap(values[distance], axis, distance)
    return [held[distance] for distance in range(size)]


def sum_rows(values, axis):
    size = lax.axis_size(axis)
    far = size // 2
    beside = {distance: swap(values[distance], axis, 1) for distance in range(far + 1, size, 2)}
    arrived = [swap(values[distance], axis, distance) for distance in list(range(2, far, 2)) + list(range(1, far, 2))]
    for distance in range(far, size, 2):
        joined = values[distance].astype(F32) + beside[distance + 1].astype(F32)
        arrived.append(swap(joined.astype(BF), axis, distance))
    total = values[0].astype(F32)
    for value in arrived:
        total = total + value.astype(F32)
    return total


def cost(micros):
    return pl.CostEstimate(flops=int(micros * 1e9), bytes_accessed=int(micros * 3e6), transcendentals=0)


def project_rows(normed, weight):
    return lax.dot_general(normed, weight, (((1,), (1,)), ((), ())), preferred_element_type=F32)


def dot(left, right):
    return jnp.dot(left, right, preferred_element_type=F32)


def rotate(values, cosines, sines):
    width = values.shape[1]
    low = iota((1, 2 * HD), 1) % HD < HD // 2
    pieces = []
    for start in range(0, width, 2 * HD):
        tile = values[:, start : start + 2 * HD]
        short = 2 * HD - tile.shape[1]
        if short:
            tile = jnp.concatenate([tile, tile], 1)
        turned = jnp.where(low, pltpu.roll(tile, 2 * HD - HD // 2, 1), pltpu.roll(tile, HD // 2, 1))
        pieces.append((tile * cosines + turned * sines)[:, : 2 * HD - short])
    return pieces[0] if len(pieces) == 1 else jnp.concatenate(pieces, 1)


def table_kernel(req_ref, length_ref, frequency_ref, cosines_ref, sines_ref):
    rows, width = cosines_ref.shape
    lengths = jnp.broadcast_to(length_ref[pl.ds(req_ref[0], 1), :].astype(F32), (rows, rows))
    lengths = jnp.where(iota((rows, rows), 0) == iota((rows, rows), 1), lengths, 0.0)
    angles = jnp.sum(lengths, -1, keepdims=True) * frequency_ref[...]
    cosines_ref[...] = jnp.cos(angles)
    sines = jnp.sin(angles)
    sines_ref[...] = jnp.where(iota((rows, width), 1) % HD < HD // 2, -sines, sines)


def query_kernel(hidden_ref, gain_ref, weight_ref, cosines_ref, sines_ref, query_ref, normed_ref):
    hidden = hidden_ref[...].astype(F32)
    scale = lax.rsqrt(jnp.mean(hidden * hidden, -1, keepdims=True) + 1e-05)
    normed = (hidden * scale * gain_ref[...]).astype(BF)
    normed_ref[...] = normed
    query = project_rows(normed, weight_ref[...])
    query_ref[...] = (rotate(query, cosines_ref[...], sines_ref[...]) * 0.125).astype(BF)


def fresh_kernel(normed_ref, key_weight_ref, value_weight_ref, cosines_ref, sines_ref, key_ref, value_ref):
    key = project_rows(normed_ref[...], key_weight_ref[...])
    key_ref[...] = rotate(key, cosines_ref[...], sines_ref[...]).astype(BF)
    value_ref[...] = project_rows(normed_ref[...], value_weight_ref[...]).astype(BF)


def attend_kernel(heads, groups, chunk, nq, *refs):
    qrow_ref, left_ref, slot_ref, local_ref = refs[:4]
    query_refs = refs[4:4+nq]
    key_ref, value_ref = refs[4 + nq : 6 + nq]
    out_refs = refs[6 + nq : -5]
    asked_ref, laid_ref, mean_ref, level_ref, rows_ref = refs[-5:]
    blocks = qrow_ref.shape[0]
    lanes = key_ref.shape[1]
    share, width = out_refs[0].shape
    per_group = heads // groups
    feature = heads * HD
    index = pl.program_id(0)

    @pl.when(index == 0)
    def _():
        total = None
        for place, query_ref in enumerate(query_refs):
            count = query_ref.shape[0]
            picked = (iota((blocks, count), 1) + place * count == qrow_ref[...]).astype(BF)
            part = dot(picked, query_ref[...])
            total = part if total is None else total + part
        asked_ref[...] = total
        laid_ref[...] = jnp.zeros(laid_ref.shape, F32)

    base = pl.multiple_of(index * chunk, chunk)
    rows = pl.ds(base, chunk)
    low = iota((chunk, 2 * HD), 1) < HD
    for pair in range((heads + 1) // 2):
        stop = min(feature, (pair + 1) * 2 * HD)
        tile = asked_ref[rows, pair * 2 * HD : stop]
        if tile.shape[1] < 2 * HD:
            tile = jnp.concatenate([tile, tile], 1)
        turned = pltpu.roll(tile, HD, 1)
        for odd in range(2):
            head = 2 * pair + odd
            if head < heads:
                first, second = (turned, tile) if odd else (tile, turned)
                laid_ref[pl.ds(head, chunk, 16), :] = jnp.where(low, first, 0.0)
                laid_ref[pl.ds(head + 8, chunk, 16), :] = jnp.where(low, 0.0, second)
    query = laid_ref[...].astype(BF)
    scores = lax.dot_general(
        query.reshape(chunk // 2, 32, 2 * HD), key_ref[...].reshape(chunk // 2, 2 * lanes, 2 * HD),
        (((2,), (2,)), ((0,), (0,))), preferred_element_type=F32)
    scores = jnp.concatenate([scores[:, None, :16, :lanes], scores[:, None, 16:, lanes:]], 1).reshape(chunk, 16, lanes)
    cell_row = iota((8, lanes), 0)
    cell_lane = iota((8, lanes), 1)
    position = jnp.where(cell_lane % groups == cell_row // per_group, 2 * (cell_lane // groups), 1 << 20)
    position = position.astype(F32)[None]
    spread = (iota((chunk * 8, chunk), 0) // 8 == iota((chunk * 8, chunk), 1)).astype(BF)
    remaining = jnp.broadcast_to(left_ref[...].astype(F32), (chunk, lanes)).astype(BF)
    remaining = dot(spread, remaining).reshape(chunk, 8, lanes)
    usable = jnp.concatenate([position < remaining, position + 1.0 < remaining], 1)
    scores = jnp.where(usable, scores, NEG)
    highest = jnp.max(jnp.maximum(scores[:, :8], scores[:, 8:]), -1, keepdims=True)
    weights = jnp.where(usable, jnp.exp(scores - jnp.concatenate([highest, highest], 1)), 0.0)
    total = jnp.sum(weights[:, :8] + weights[:, 8:], -1, keepdims=True)
    weights = weights.astype(BF).reshape(chunk // 2, 2, 16, lanes)
    none = jnp.zeros((chunk // 2, 16, lanes), BF)
    weights = jnp.concatenate([jnp.concatenate([weights[:, 0], none], 2), jnp.concatenate([none, weights[:, 1]], 2)], 1)
    numer = lax.dot_general(weights, value_ref[...].reshape(chunk // 2, 2 * lanes, 2 * HD), (((2,), (1,)), ((0,), (0,))), preferred_element_type=F32)
    numer = numer.reshape(chunk, 16, 2 * HD)
    numer = jnp.where(iota((1, 8, 2 * HD), 2) < HD, numer[:, :8], numer[:, 8:]).reshape(chunk * 8, 2 * HD)
    numer = numer + pltpu.roll(numer, HD, 1)
    total = total.reshape(chunk * 8, 1)
    highest = highest.reshape(chunk * 8, 1)
    some = total > 0.0
    safe = jnp.where(some, total, 1.0)
    mean_ref[...] = numer / safe
    level_ref[...] = jnp.broadcast_to(jnp.where(some, highest + jnp.log(safe), NEG), (chunk * 8, 2 * HD))
    lane = iota((chunk, 2 * HD), 1)
    means = [mean_ref[pl.ds(head, chunk, 8), :] for head in range(heads)]
    extras = jnp.zeros((chunk, 2 * HD), F32)
    start = feature % (2 * HD)
    for head in range(heads):
        level = level_ref[pl.ds(head, chunk, 8), :]
        first = level.astype(BF).astype(F32)
        second = (level - first).astype(BF).astype(F32)
        third = level - first - second
        for part, piece in enumerate((first, second, third)):
            extras = jnp.where(lane == start + 4 * head + part, piece, extras)
    extras = jnp.where(lane == start + HD - 1, local_ref[...].astype(F32), extras)
    for pair in range(width // (2 * HD)):
        left = means[2 * pair] if 2 * pair < heads else extras
        right = means[2 * pair + 1] if 2 * pair + 1 < heads else extras
        rows_ref[rows, pair * 2 * HD : (pair + 1) * 2 * HD] = jnp.where(low, left, right).astype(BF)

    @pl.when(index == blocks // chunk - 1)
    def _():
        order = (slot_ref[...] == iota((blocks, blocks), 0)).astype(BF)
        sorted_rows = dot(order, rows_ref[...])
        for place, out_ref in enumerate(out_refs):
            out_ref[...] = sorted_rows[place * share : (place + 1) * share].astype(BF)

def attend(heads, groups, chunk, width, qrow, left, slot, local, queries, keys, values, limit=24):
    blocks, lanes = keys.shape[:2]
    whole = pl.BlockSpec(memory_space=pltpu.VMEM)
    block = lambda *shape: pl.BlockSpec(shape, lambda i: (i,) + (0,) * (len(shape) - 1))
    return pl.pallas_call(
        functools.partial(attend_kernel, heads, groups, chunk, len(queries)),
        grid=(blocks // chunk,),
        out_shape=[jax.ShapeDtypeStruct((blocks // len(queries), width), BF)] * len(queries),
        in_specs=[whole, block(chunk, 1), whole, block(chunk, 1)] + [whole] * len(queries)
        + [block(chunk, lanes, 2 * HD)] * 2,
        out_specs=[whole] * len(queries),
        scratch_shapes=[
            pltpu.VMEM((blocks, heads * HD), F32),
            pltpu.VMEM((chunk * 16, 2 * HD), F32),
            pltpu.VMEM((chunk * 8, 2 * HD), F32),
            pltpu.VMEM((chunk * 8, 2 * HD), F32),
            pltpu.VMEM((blocks, width), BF),
        ],
        compiler_params=pltpu.CompilerParams(vmem_limit_bytes=limit << 20),
        cost_estimate=cost(COSTS[2]),
        name="attend",
    )(qrow, left, slot, local, *queries, keys, values)


def merge_kernel(heads, groups, tokens, *refs):
    kv_ref, query_ref, key_ref, value_ref, weight_ref = refs[:5]
    out_refs = refs[-1 - tokens : -1]
    result_ref = refs[-1]
    part_refs = refs[5 : -1 - tokens]
    parts = jnp.concatenate([part_ref[...] for part_ref in part_refs], 0)
    rows = query_ref.shape[0]
    blocks, width = parts.shape
    per_group = heads // groups
    feature = heads * HD
    row = iota((32, width), 0)
    column = iota((32, width), 1) - feature
    wanted = jnp.where(row < 24, (row % 8) * 4 + row // 8, HD - 1)
    pick = jnp.logical_and(column == wanted, jnp.logical_or(row == 24, row % 8 < heads))
    pick = jnp.logical_and(pick, row <= 24).astype(BF)
    extras = lax.dot_general(pick, parts, (((1,), (1,)), ((), ())), preferred_element_type=F32)
    levels = extras[0:8] + extras[8:16] + extras[16:24]
    local = extras[24:25].astype(jnp.int32)
    member = local == iota((rows, blocks), 0)

    source = iota((groups * HD, width), 0)
    target = iota((groups * HD, width), 1)
    same = jnp.logical_and(source // HD == target // (HD * per_group), source % HD == target % HD)
    widen = same.astype(BF)
    key = dot(key_ref[...], widen)
    value = dot(value_ref[...], widen)
    products = query_ref[...].astype(F32) * key[:, :feature]
    lane_head = iota((rows, width), 1) // HD
    joined = jnp.zeros((rows, width), F32)
    for head in range(heads):
        own = jnp.sum(jnp.where(lane_head[:, :feature] == head, products, 0.0), -1, keepdims=True)
        level = levels[head : head + 1]
        highest = jnp.max(jnp.where(member, level, NEG), -1, keepdims=True)
        highest = jnp.maximum(highest, own)
        weights = jnp.where(member, jnp.exp(level - highest), 0.0).astype(BF)
        own_weight = jnp.exp(own - highest)
        total = jnp.sum(weights.astype(F32), -1, keepdims=True) + own_weight
        numer = dot(weights, parts) + own_weight * value
        joined = jnp.where(lane_head == head, numer / total, joined)
    attended = joined[:, :feature].astype(BF)
    result_ref[...] = dot(attended, weight_ref[...])
    count = rows // tokens
    for place, out_ref in enumerate(out_refs):
        start = pl.multiple_of(jnp.bitwise_xor(kv_ref[0], place) * count, count)
        out_ref[...] = result_ref[pl.ds(start, count), :].astype(BF)


def route_kernel(kv_ref, hidden_ref, gain_ref, router_ref, routes_ref, *refs):
    piece_refs = refs[:-2]
    after_ref, out_ref = refs[-2:]
    count, model = after_ref.shape
    start = pl.multiple_of(kv_ref[0] * count, count)
    total = piece_refs[0][...].astype(F32)
    for piece_ref in piece_refs[1:]:
        total = total + piece_ref[...].astype(F32)
    after = hidden_ref[pl.ds(start, count), :].astype(F32) + total
    after_ref[...] = after
    scale = lax.rsqrt(jnp.mean(after * after, -1, keepdims=True) + 1e-05)
    normed = (after * scale * gain_ref[...]).astype(BF)
    out_ref[:, :model] = normed
    experts = router_ref.shape[1]
    logits = dot(normed, router_ref[...])
    expert = iota((count, experts), 1)
    chosen = expert == routes_ref[:, 0:1]
    for turn in range(1, routes_ref.shape[1]):
        chosen = jnp.logical_or(chosen, expert == routes_ref[:, turn : turn + 1])
    logits = jnp.where(chosen, logits, NEG)
    gates = jnp.where(chosen, jnp.exp(logits - jnp.max(logits, -1, keepdims=True)), 0.0)
    gates = gates / jnp.sum(gates, -1, keepdims=True)
    high = gates.astype(BF).astype(F32)
    spare = jnp.zeros((count, 128 - 2 * experts), F32)
    out_ref[:, model:] = jnp.concatenate([high, gates - high, spare], 1).astype(BF)


def expert_kernel(sources, experts, req_ref, *refs):
    token_refs = refs[:sources]
    up_ref, down_ref = refs[sources : sources + 2]
    out_refs = refs[sources + 2 : -2]
    tokens_ref, mixed_ref = refs[-2:]
    index = pl.program_id(0)
    count, model = out_refs[0].shape
    hidden = down_ref.shape[1]

    @pl.when(index == 0)
    def _():
        for place, token_ref in enumerate(token_refs):
            tokens_ref[place * count : (place + 1) * count, :] = token_ref[...]

    lane = iota((sources * count, 128), 1)
    mine = req_ref[0] * pl.num_programs(0) + index
    gates = tokens_ref[:, model:].astype(F32)
    picked = jnp.logical_or(lane == mine, lane == mine + experts)
    gate = jnp.sum(jnp.where(picked, gates, 0.0), -1, keepdims=True)
    both = dot(tokens_ref[:, :model], up_ref[0])
    active = (jax.nn.silu(both[:, :hidden]) * both[:, hidden:]).astype(BF)
    produced = dot(active, down_ref[0]).astype(BF).astype(F32) * gate

    @pl.when(index == 0)
    def _():
        mixed_ref[...] = produced

    @pl.when(index > 0)
    def _():
        mixed_ref[...] += produced

    @pl.when(index == pl.num_programs(0) - 1)
    def _():
        for place, out_ref in enumerate(out_refs):
            out_ref[...] = mixed_ref[place * count : (place + 1) * count, :].astype(BF)


def shards(
    hidden_in,
    attn_gain,
    w_query,
    w_key,
    w_value,
    w_out,
    k_cache,
    v_cache,
    cache_len,
    block_slot,
    moe_gain,
    w_router,
    w_gate_up,
    w_down,
    routes,
):
    req_index = lax.axis_index("req")
    kv_index = lax.axis_index("kv")
    sources = lax.axis_size("req")
    kv_size = lax.axis_size("kv")
    row_count, model = hidden_in.shape
    heads = w_query.shape[0] // HD
    groups = w_key.shape[0] // HD
    blocks = k_cache.shape[0]
    requests = cache_len.shape[0]
    share = blocks // sources
    width = -(-(heads * HD + HD) // 128) * 128

    vmem = pl.BlockSpec(memory_space=pltpu.VMEM)
    scalar = pl.BlockSpec(memory_space=pltpu.SMEM)
    req_scalar = jnp.reshape(req_index, (1,)).astype(jnp.int32)
    frequency = 10000.0 ** (-(np.arange(2 * HD) % (HD // 2)) / (HD // 2))
    cosines, sines = pl.pallas_call(
        table_kernel,
        out_shape=[jax.ShapeDtypeStruct((row_count, 2 * HD), F32)] * 2,
        in_specs=[scalar, vmem, vmem],
        out_specs=[vmem] * 2,
        compiler_params=pltpu.CompilerParams(vmem_limit_bytes=4 << 20),
        cost_estimate=cost(COSTS[6]),
        name="tables",
    )(req_scalar, cache_len.reshape(sources, row_count), jnp.asarray(frequency[None, :], F32))
    query, normed = pl.pallas_call(
        query_kernel,
        out_shape=[
            jax.ShapeDtypeStruct((row_count, heads * HD), BF),
            jax.ShapeDtypeStruct((row_count, model), BF),
        ],
        in_specs=[vmem] * 5,
        out_specs=[vmem] * 2,
        cost_estimate=cost(COSTS[0]),
        compiler_params=pltpu.CompilerParams(vmem_limit_bytes=8 << 20),
        name="query",
    )(hidden_in, attn_gain[None, :], w_query, cosines, sines)
    key_new, value_new = pl.pallas_call(
        fresh_kernel,
        out_shape=[jax.ShapeDtypeStruct((row_count, groups * HD), BF)] * 2,
        in_specs=[vmem] * 5,
        out_specs=[vmem] * 2,
        cost_estimate=cost(COSTS[1]),
        compiler_params=pltpu.CompilerParams(vmem_limit_bytes=8 << 20),
        name="fresh",
    )(normed, w_key, w_value, cosines, sines)
    queries = gather_rows(query, "req")

    owners = block_slot // PAGES
    home = owners // row_count
    local = owners % row_count
    owned = owners[:, None] == jnp.arange(requests, dtype=jnp.int32)[None, :]
    lengths = jnp.sum(jnp.where(owned, cache_len[None, :], 0), 1)
    left = lengths - (block_slot % PAGES) * BLK
    left = jnp.clip(left, 0, BLK)
    number = jnp.arange(blocks, dtype=jnp.int32)
    earlier = jnp.logical_and(home[:, None] == home[None, :], number[:, None] < number[None, :])
    rank = jnp.sum(earlier.astype(jnp.int32), 0)
    place = jnp.bitwise_xor(home, req_index)
    slot = place * share + rank
    query_row = place * row_count + local

    def pairs(cache):
        cache = cache.reshape(blocks, groups, HD, 2 * HD).transpose(0, 2, 1, 3)
        return cache.reshape(blocks, HD * groups, 2 * HD)

    partial = attend(
        heads, groups, CHUNK, width, query_row[:, None], left[:, None], slot[None, :], local[:, None],
        queries, pairs(k_cache), pairs(v_cache),
    )
    parts = send_rows(partial, "req")
    kv_scalar = jnp.reshape(kv_index, (1,)).astype(jnp.int32)
    token_count = row_count // kv_size
    projected = pl.pallas_call(
        functools.partial(merge_kernel, heads, groups, kv_size),
        out_shape=[jax.ShapeDtypeStruct((token_count, model), BF)] * kv_size,
        in_specs=[scalar] + [vmem] * (4 + sources),
        out_specs=[vmem] * kv_size,
        scratch_shapes=[pltpu.VMEM((row_count, model), F32)],
        compiler_params=pltpu.CompilerParams(vmem_limit_bytes=10 << 20),
        cost_estimate=cost(COSTS[3]),
        name="merge",
    )(kv_scalar, query, key_new, value_new, w_out, *parts)
    pieces = [projected[0]]
    for distance in range(1, kv_size):
        pieces.append(swap(projected[distance], "kv", distance))
    after_attn, outgoing = pl.pallas_call(
        route_kernel,
        out_shape=[
            jax.ShapeDtypeStruct((token_count, model), F32),
            jax.ShapeDtypeStruct((token_count, model + 128), BF),
        ],
        in_specs=[scalar] + [vmem] * (4 + kv_size),
        out_specs=[vmem, vmem],
        compiler_params=pltpu.CompilerParams(vmem_limit_bytes=10 << 20),
        cost_estimate=cost(COSTS[4]),
        name="route",
    )(kv_scalar, hidden_in, moe_gain[None, :], w_router, routes, *pieces)
    arrived = gather_rows(outgoing, "req")
    local_experts = w_gate_up.shape[0]
    mixed = pl.pallas_call(
        functools.partial(expert_kernel, sources, w_router.shape[1]),
        grid=(local_experts,),
        out_shape=[jax.ShapeDtypeStruct((token_count, model), BF)] * sources,
        in_specs=[scalar]
        + [vmem] * sources
        + [
            pl.BlockSpec((1,) + w_gate_up.shape[1:], lambda i: (i, 0, 0)),
            pl.BlockSpec((1,) + w_down.shape[1:], lambda i: (i, 0, 0)),
        ],
        out_specs=[vmem] * sources,
        scratch_shapes=[
            pltpu.VMEM((sources * token_count, model + 128), BF),
            pltpu.VMEM((sources * token_count, model), F32),
        ],
        compiler_params=pltpu.CompilerParams(vmem_limit_bytes=24 << 20),
        cost_estimate=cost(COSTS[5]),
        name="experts",
    )(req_scalar, *arrived, w_gate_up, w_down)
    mixture = sum_rows(mixed, "req")
    return (after_attn + mixture).astype(BF)


def solution(mesh):
    placed = (
        P("req", None),
        P(),
        P("kv", None),
        P("kv", None),
        P("kv", None),
        P("kv", None),
        P("req", "kv", None),
        P("req", "kv", None),
        P(),
        P("req"),
        P(),
        P(),
        P("req", None, None),
        P("req", None, None),
        P(("req", "kv"), None),
    )
    return jax.shard_map(
        shards, mesh=mesh, in_specs=placed, out_specs=P(("req", "kv"), None), check_vma=False
    )
```

```python
import functools
import math

import jax
import jax.numpy as jnp
from jax import lax
from jax.experimental import pallas as pl
from jax.experimental.pallas import tpu as pltpu
from jax.sharding import PartitionSpec as P

HD = 64
FFE = 512
BLK = 128
PAGES = 3
CHUNK = 96
QLIM = 60
ALIM = 24
SLIM = 1
STAGE = True
COSTS = (12.0, 1.0, 12.0, 12.0, 12.0, 4.0, 12.0)
NEG = -1e30
BF = jnp.bfloat16
F32 = jnp.float32


def iota(shape, dim):
    return lax.broadcasted_iota(jnp.int32, shape, dim)


def swap(value, axis, distance):
    size = lax.axis_size(axis)
    return lax.ppermute(value, axis, [(source, source ^ distance) for source in range(size)])


def gather_rows(value, axis):
    size = lax.axis_size(axis)
    held = {0: value}
    far = size // 2
    for distance in list(range(far, size, 2)) + list(range(2, far, 2)) + list(range(1, far, 2)):
        held[distance] = swap(value, axis, distance)
    for distance in range(far + 1, size, 2):
        held[distance] = swap(held[distance - 1], axis, 1)
    return [held[distance] for distance in range(size)]


def send_rows(values, axis):
    size = lax.axis_size(axis)
    held = {0: values[0]}
    far = size // 2
    for start in list(range(size - 2, far - 1, -2)) + list(range(2, far, 2)) + [0]:
        for distance in (start, start + 1):
            if distance:
                held[distance] = swap(values[distance], axis, distance)
    return [held[distance] for distance in sorted(held, key=lambda distance: -distance)]


def sum_rows(values, axis):
    size = lax.axis_size(axis)
    far = size // 2
    split = far + far // 2
    beside = {distance: swap(values[distance], axis, 1) for distance in range(split + 1, size, 2)}
    arrived = [swap(values[distance], axis, distance) for distance in range(far, split)]
    arrived += [swap(values[distance], axis, distance) for distance in range(2, far, 2)]
    joined = {}
    for distance in range(split, size, 2):
        both = values[distance].astype(F32) + beside[distance + 1].astype(F32)
        joined[distance] = both.astype(BF)
    odd = {distance: values[distance] for distance in range(1, far, 2)}
    joined, odd = lax.optimization_barrier((joined, odd))
    arrived += [swap(value, axis, distance) for distance, value in joined.items()]
    arrived += [swap(value, axis, distance) for distance, value in odd.items()]
    total = values[0].astype(F32)
    for value in arrived:
        total = total + value.astype(F32)
    return total


def cost(micros):
    return pl.CostEstimate(flops=int(micros * 1e9), bytes_accessed=int(micros * 3e6), transcendentals=0)


def project_rows(normed, weight):
    return lax.dot_general(normed, weight, (((1,), (1,)), ((), ())), preferred_element_type=F32)


def dot(left, right):
    return jnp.dot(left, right, preferred_element_type=F32)


def rotate(values, cosines, sines):
    width = values.shape[1]
    low = iota((1, 2 * HD), 1) % HD < HD // 2
    pieces = []
    for start in range(0, width, 2 * HD):
        tile = values[:, start : start + 2 * HD]
        short = 2 * HD - tile.shape[1]
        if short:
            tile = jnp.concatenate([tile, tile], 1)
        turned = jnp.where(low, pltpu.roll(tile, 2 * HD - HD // 2, 1), pltpu.roll(tile, HD // 2, 1))
        pieces.append((tile * cosines + turned * sines)[:, : 2 * HD - short])
    return pieces[0] if len(pieces) == 1 else jnp.concatenate(pieces, 1)


def query_kernel(req_ref, hidden_hbm, gain_hbm, weight_hbm, length_hbm, query_ref, normed_ref, cosines_ref,
                 sines_ref, hidden_ref, gain_ref, weight_ref, length_ref, sem):
    copies = [
        pltpu.make_async_copy(source, target, sem.at[place])
        for place, (source, target) in enumerate(
            [(length_hbm, length_ref), (hidden_hbm, hidden_ref), (weight_hbm, weight_ref), (gain_hbm, gain_ref)]
        )
    ]
    for copy in copies:
        copy.start()
    rows = cosines_ref.shape[0]
    copies[0].wait()
    lengths = jnp.broadcast_to(length_ref[pl.ds(req_ref[0], 1), :].astype(F32), (rows, rows))
    lengths = jnp.where(iota((rows, rows), 0) == iota((rows, rows), 1), lengths, 0.0)
    exponent = (iota((1, 2 * HD), 1) % (HD // 2)).astype(F32) * (-2.0 / HD)
    angles = jnp.sum(lengths, -1, keepdims=True) * jnp.exp(exponent * math.log(10000.0))
    cosines = jnp.cos(angles)
    sines = jnp.sin(angles)
    sines = jnp.where(iota((1, 2 * HD), 1) % HD < HD // 2, -sines, sines)
    cosines_ref[...] = cosines
    sines_ref[...] = sines
    copies[1].wait()
    hidden = hidden_ref[...].astype(F32)
    scale = lax.rsqrt(jnp.mean(hidden * hidden, -1, keepdims=True) + 1e-05)
    copies[3].wait()
    normed = (hidden * scale * lanes_of(gain_ref)).astype(BF)
    normed_ref[...] = normed
    copies[2].wait()
    query = project_rows(normed, weight_ref[...])
    query_ref[...] = (rotate(query, cosines, sines) * 0.125).astype(BF)


def place_kernel(rows, share, req_ref, block_ref, length_ref, query_ref, left_ref, slot_ref, local_ref):
    blocks = block_ref.shape[1]
    here = iota((blocks, blocks), 0)
    there = iota((blocks, blocks), 1)
    by_lane = block_ref[...]
    by_row = jnp.sum(jnp.where(here == there, by_lane, 0), 1, keepdims=True)
    owner = by_row // PAGES
    home = owner // rows
    local_ref[...] = owner % rows
    query_ref[...] = jnp.bitwise_xor(home, req_ref[0]) * rows + owner % rows
    lengths = lanes_of(length_ref)
    owned = owner == iota((blocks, lengths.shape[1]), 1)
    left = jnp.sum(jnp.where(owned, lengths, 0), 1, keepdims=True) - (by_row - owner * PAGES) * BLK
    left_ref[...] = jnp.sum(jnp.where(here == there, left, 0), 0, keepdims=True)
    lane_home = by_lane // PAGES // rows
    earlier = jnp.logical_and(home == lane_home, here < there)
    rank = jnp.sum(earlier.astype(jnp.int32), 0, keepdims=True)
    slot_ref[...] = jnp.bitwise_xor(lane_home, req_ref[0]) * share + rank


def lanes_of(ref):
    return jnp.concatenate([ref[row : row + 1, :] for row in range(ref.shape[0])], 1)


def fresh_kernel(normed_ref, key_weight_ref, value_weight_ref, cosines_ref, sines_ref, key_ref, value_ref):
    key = project_rows(normed_ref[...], key_weight_ref[...])
    key_ref[...] = rotate(key, cosines_ref[...], sines_ref[...]).astype(BF)
    value_ref[...] = project_rows(normed_ref[...], value_weight_ref[...]).astype(BF)


def attend_kernel(heads, groups, chunk, nq, *refs):
    qrow_ref, left_ref, slot_ref, local_ref = refs[:4]
    query_refs = refs[4:4+nq]
    key_ref, value_ref = refs[4 + nq : 6 + nq]
    out_refs = refs[6 + nq : -5]
    asked_ref, laid_ref, mean_ref, level_ref, rows_ref = refs[-5:]
    blocks = qrow_ref.shape[0]
    lanes = key_ref.shape[1]
    share, width = out_refs[0].shape
    per_group = heads // groups
    feature = heads * HD
    index = pl.program_id(0)

    @pl.when(index == 0)
    def _():
        total = None
        for place, query_ref in enumerate(query_refs):
            count = query_ref.shape[0]
            picked = (iota((blocks, count), 1) + place * count == qrow_ref[...]).astype(BF)
            part = dot(picked, query_ref[...])
            total = part if total is None else total + part
        asked_ref[...] = total
        laid_ref[...] = jnp.zeros(laid_ref.shape, F32)

    base = pl.multiple_of(index * chunk, chunk)
    rows = pl.ds(base, chunk)
    low = iota((chunk, 2 * HD), 1) < HD
    for pair in range((heads + 1) // 2):
        stop = min(feature, (pair + 1) * 2 * HD)
        tile = asked_ref[rows, pair * 2 * HD : stop]
        if tile.shape[1] < 2 * HD:
            tile = jnp.concatenate([tile, tile], 1)
        turned = pltpu.roll(tile, HD, 1)
        for odd in range(2):
            head = 2 * pair + odd
            if head < heads:
                first, second = (turned, tile) if odd else (tile, turned)
                laid_ref[pl.ds(head, chunk, 16), :] = jnp.where(low, first, 0.0)
                laid_ref[pl.ds(head + 8, chunk, 16), :] = jnp.where(low, 0.0, second)
    query = laid_ref[: chunk * 16, :].astype(BF)
    scores = lax.dot_general(
        query.reshape(chunk // 2, 32, 2 * HD), key_ref[...].reshape(chunk // 2, 2 * lanes, 2 * HD),
        (((2,), (2,)), ((0,), (0,))), preferred_element_type=F32)
    scores = jnp.concatenate([scores[:, None, :16, :lanes], scores[:, None, 16:, lanes:]], 1).reshape(chunk, 16, lanes)
    cell_row = iota((8, lanes), 0)
    cell_lane = iota((8, lanes), 1)
    position = jnp.where(cell_lane % groups == cell_row // per_group, 2 * (cell_lane // groups), 1 << 20)
    position = position[None]
    remaining = [jnp.full((1, 8, lanes), left_ref[0, base + place], jnp.int32) for place in range(chunk)]
    remaining = jnp.concatenate(remaining, 0)
    usable = jnp.concatenate([position < remaining, position + 1 < remaining], 1)
    scores = jnp.where(usable, scores, NEG)
    highest = jnp.max(jnp.maximum(scores[:, :8], scores[:, 8:]), -1, keepdims=True)
    weights = jnp.where(usable, jnp.exp(scores - jnp.concatenate([highest, highest], 1)), 0.0)
    total = jnp.sum(weights[:, :8] + weights[:, 8:], -1, keepdims=True)
    weights = weights.astype(BF).reshape(chunk // 2, 2, 16, lanes)
    none = jnp.zeros((chunk // 2, 16, lanes), BF)
    weights = jnp.concatenate([jnp.concatenate([weights[:, 0], none], 2), jnp.concatenate([none, weights[:, 1]], 2)], 1)
    numer = lax.dot_general(weights, value_ref[...].reshape(chunk // 2, 2 * lanes, 2 * HD), (((2,), (1,)), ((0,), (0,))), preferred_element_type=F32)
    numer = numer.reshape(chunk, 16, 2 * HD)
    numer = jnp.where(iota((1, 8, 2 * HD), 2) < HD, numer[:, :8], numer[:, 8:]).reshape(chunk * 8, 2 * HD)
    numer = numer + pltpu.roll(numer, HD, 1)
    total = total.reshape(chunk * 8, 1)
    highest = highest.reshape(chunk * 8, 1)
    some = total > 0.0
    safe = jnp.where(some, total, 1.0)
    mean_ref[: chunk * 8, :] = numer / safe
    level_ref[: chunk * 8, :] = jnp.broadcast_to(jnp.where(some, highest + jnp.log(safe), NEG), (chunk * 8, 2 * HD))
    lane = iota((chunk, 2 * HD), 1)
    means = [mean_ref[pl.ds(head, chunk, 8), :] for head in range(heads)]
    extras = jnp.zeros((chunk, 2 * HD), F32)
    start = feature % (2 * HD)
    for head in range(heads):
        level = level_ref[pl.ds(head, chunk, 8), :]
        first = level.astype(BF).astype(F32)
        second = (level - first).astype(BF).astype(F32)
        third = level - first - second
        for part, piece in enumerate((first, second, third)):
            extras = jnp.where(lane == start + 4 * head + part, piece, extras)
    extras = jnp.where(lane == start + HD - 1, local_ref[...].astype(F32), extras)
    for pair in range(width // (2 * HD)):
        left = means[2 * pair] if 2 * pair < heads else extras
        right = means[2 * pair + 1] if 2 * pair + 1 < heads else extras
        rows_ref[rows, pair * 2 * HD : (pair + 1) * 2 * HD] = jnp.where(low, left, right).astype(BF)

    @pl.when(index == blocks // chunk - 1)
    def _():
        order = (slot_ref[...] == iota((blocks, blocks), 0)).astype(BF)
        sorted_rows = dot(order, rows_ref[...])
        for place, out_ref in enumerate(out_refs):
            out_ref[...] = sorted_rows[place * share : (place + 1) * share].astype(BF)

def attend(heads, groups, chunk, width, qrow, left, slot, local, queries, keys, values, limit=ALIM):
    blocks, lanes = keys.shape[:2]
    whole = pl.BlockSpec(memory_space=pltpu.VMEM)
    block = lambda *shape: pl.BlockSpec(shape, lambda i: (i,) + (0,) * (len(shape) - 1))
    return pl.pallas_call(
        functools.partial(attend_kernel, heads, groups, chunk, len(queries)),
        grid=(blocks // chunk,),
        out_shape=[jax.ShapeDtypeStruct((blocks // len(queries), width), BF)] * len(queries),
        in_specs=[whole, pl.BlockSpec(memory_space=pltpu.SMEM), whole, block(chunk, 1)] + [whole] * len(queries)
        + [block(chunk, lanes, 2 * HD)] * 2,
        out_specs=[whole] * len(queries),
        scratch_shapes=[
            pltpu.VMEM((blocks, heads * HD), F32),
            pltpu.VMEM((chunk * 16 + 16, 2 * HD), F32),
            pltpu.VMEM((chunk * 8 + 8, 2 * HD), F32),
            pltpu.VMEM((chunk * 8 + 8, 2 * HD), F32),
            pltpu.VMEM((blocks, width), BF),
        ],
        compiler_params=pltpu.CompilerParams(vmem_limit_bytes=limit << 20),
        cost_estimate=cost(COSTS[2]),
        name="attend",
    )(qrow, left, slot, local, *queries, keys, values)


def merge_kernel(heads, groups, tokens, *refs):
    kv_ref, query_ref, key_ref, value_ref, weight_ref = refs[:5]
    out_refs = refs[-1 - tokens : -1]
    result_ref = refs[-1]
    part_refs = refs[5 : -1 - tokens]
    parts = jnp.concatenate([part_ref[...] for part_ref in part_refs], 0)
    rows = query_ref.shape[0]
    blocks, width = parts.shape
    per_group = heads // groups
    feature = heads * HD
    row = iota((32, width), 0)
    column = iota((32, width), 1) - feature
    wanted = jnp.where(row < 24, (row % 8) * 4 + row // 8, HD - 1)
    pick = jnp.logical_and(column == wanted, jnp.logical_or(row == 24, row % 8 < heads))
    pick = jnp.logical_and(pick, row <= 24).astype(BF)
    extras = lax.dot_general(pick, parts, (((1,), (1,)), ((), ())), preferred_element_type=F32)
    levels = extras[0:8] + extras[8:16] + extras[16:24]
    local = extras[24:25].astype(jnp.int32)
    member = local == iota((rows, blocks), 0)

    source = iota((groups * HD, width), 0)
    target = iota((groups * HD, width), 1)
    same = jnp.logical_and(source // HD == target // (HD * per_group), source % HD == target % HD)
    widen = same.astype(BF)
    key = dot(key_ref[...], widen)
    value = dot(value_ref[...], widen)
    products = query_ref[...].astype(F32) * key[:, :feature]
    lane_head = iota((rows, width), 1) // HD
    joined = jnp.zeros((rows, width), F32)
    for head in range(heads):
        own = jnp.sum(jnp.where(lane_head[:, :feature] == head, products, 0.0), -1, keepdims=True)
        level = levels[head : head + 1]
        highest = jnp.max(jnp.where(member, level, NEG), -1, keepdims=True)
        highest = jnp.maximum(highest, own)
        weights = jnp.where(member, jnp.exp(level - highest), 0.0).astype(BF)
        own_weight = jnp.exp(own - highest)
        total = jnp.sum(weights.astype(F32), -1, keepdims=True) + own_weight
        numer = dot(weights, parts) + own_weight * value
        joined = jnp.where(lane_head == head, numer / total, joined)
    attended = joined[:, :feature].astype(BF)
    result_ref[...] = dot(attended, weight_ref[...])
    count = rows // tokens
    for place, out_ref in enumerate(out_refs):
        start = pl.multiple_of(jnp.bitwise_xor(kv_ref[0], place) * count, count)
        out_ref[...] = result_ref[pl.ds(start, count), :].astype(BF)


def route_kernel(kv_ref, hidden_ref, gain_ref, router_ref, routes_ref, *refs):
    piece_refs = refs[:-2]
    after_ref, out_ref = refs[-2:]
    count, model = after_ref.shape
    start = pl.multiple_of(kv_ref[0] * count, count)
    total = piece_refs[0][...].astype(F32)
    for piece_ref in piece_refs[1:]:
        total = total + piece_ref[...].astype(F32)
    after = hidden_ref[pl.ds(start, count), :].astype(F32) + total
    after_ref[...] = after
    scale = lax.rsqrt(jnp.mean(after * after, -1, keepdims=True) + 1e-05)
    normed = (after * scale * lanes_of(gain_ref)).astype(BF)
    out_ref[:, :model] = normed
    experts = router_ref.shape[1]
    logits = dot(normed, router_ref[...])
    expert = iota((count, experts), 1)
    chosen = expert == routes_ref[:, 0:1]
    for turn in range(1, routes_ref.shape[1]):
        chosen = jnp.logical_or(chosen, expert == routes_ref[:, turn : turn + 1])
    logits = jnp.where(chosen, logits, NEG)
    gates = jnp.where(chosen, jnp.exp(logits - jnp.max(logits, -1, keepdims=True)), 0.0)
    gates = gates / jnp.sum(gates, -1, keepdims=True)
    high = gates.astype(BF).astype(F32)
    spare = jnp.zeros((count, 128 - 2 * experts), F32)
    out_ref[:, model:] = jnp.concatenate([high, gates - high, spare], 1).astype(BF)


def stage_kernel(order_ref, source_ref, target_ref, sem):
    copy = pltpu.make_async_copy(source_ref, target_ref, sem)
    copy.start()
    copy.wait()


def expert_kernel(sources, experts, req_ref, *refs):
    token_refs = refs[:sources]
    up_ref, down_ref = refs[sources : sources + 2]
    out_refs = refs[sources + 2 : -2]
    tokens_ref, mixed_ref = refs[-2:]
    index = pl.program_id(0)
    count, model = out_refs[0].shape
    hidden = down_ref.shape[1]

    @pl.when(index == 0)
    def _():
        for place, token_ref in enumerate(token_refs):
            tokens_ref[place * count : (place + 1) * count, :] = token_ref[...]

    lane = iota((sources * count, 128), 1)
    mine = req_ref[0] * pl.num_programs(0) + index
    gates = tokens_ref[:, model:].astype(F32)
    picked = jnp.logical_or(lane == mine, lane == mine + experts)
    gate = jnp.sum(jnp.where(picked, gates, 0.0), -1, keepdims=True)
    both = dot(tokens_ref[:, :model], up_ref[0])
    active = (jax.nn.silu(both[:, :hidden]) * both[:, hidden:]).astype(BF)
    produced = dot(active, down_ref[0]).astype(BF).astype(F32) * gate

    @pl.when(index == 0)
    def _():
        mixed_ref[...] = produced

    @pl.when(index > 0)
    def _():
        mixed_ref[...] += produced

    @pl.when(index == pl.num_programs(0) - 1)
    def _():
        for place, out_ref in enumerate(out_refs):
            out_ref[...] = mixed_ref[place * count : (place + 1) * count, :].astype(BF)


def shards(
    hidden_in,
    attn_gain,
    w_query,
    w_key,
    w_value,
    w_out,
    k_cache,
    v_cache,
    cache_len,
    block_slot,
    moe_gain,
    w_router,
    w_gate_up,
    w_down,
    routes,
):
    req_index = lax.axis_index("req")
    kv_index = lax.axis_index("kv")
    sources = lax.axis_size("req")
    kv_size = lax.axis_size("kv")
    row_count, model = hidden_in.shape
    heads = w_query.shape[0] // HD
    groups = w_key.shape[0] // HD
    blocks = k_cache.shape[0]
    requests = cache_len.shape[0]
    share = blocks // sources
    width = -(-(heads * HD + HD) // 128) * 128

    vmem = pl.BlockSpec(memory_space=pltpu.VMEM)
    scalar = pl.BlockSpec(memory_space=pltpu.SMEM)
    req_scalar = jnp.reshape(req_index, (1,)).astype(jnp.int32)
    far = pl.BlockSpec(memory_space=pltpu.HBM)
    query, normed, cosines, sines = pl.pallas_call(
        query_kernel,
        out_shape=[
            jax.ShapeDtypeStruct((row_count, heads * HD), BF),
            jax.ShapeDtypeStruct((row_count, model), BF),
            jax.ShapeDtypeStruct((row_count, 2 * HD), F32),
            jax.ShapeDtypeStruct((row_count, 2 * HD), F32),
        ],
        in_specs=[scalar] + [far] * 4,
        out_specs=[vmem] * 4,
        scratch_shapes=[
            pltpu.VMEM((row_count, model), BF),
            pltpu.VMEM((model // 128, 128), F32),
            pltpu.VMEM(w_query.shape, BF),
            pltpu.VMEM((sources, row_count), jnp.int32),
            pltpu.SemaphoreType.DMA((4,)),
        ],
        cost_estimate=cost(COSTS[0]),
        compiler_params=pltpu.CompilerParams(vmem_limit_bytes=QLIM << 20),
        name="query",
    )(req_scalar, hidden_in, attn_gain.reshape(-1, 128), w_query, cache_len.reshape(sources, row_count))
    key_new, value_new = pl.pallas_call(
        fresh_kernel,
        out_shape=[jax.ShapeDtypeStruct((row_count, groups * HD), BF)] * 2,
        in_specs=[vmem] * 5,
        out_specs=[vmem] * 2,
        cost_estimate=cost(COSTS[1]),
        compiler_params=pltpu.CompilerParams(vmem_limit_bytes=8 << 20),
        name="fresh",
    )(normed, w_key, w_value, cosines, sines)
    queries = gather_rows(query, "req")

    query_row, left, slot, local = pl.pallas_call(
        functools.partial(place_kernel, row_count, share),
        out_shape=[
            jax.ShapeDtypeStruct((blocks, 1), jnp.int32),
            jax.ShapeDtypeStruct((1, blocks), jnp.int32),
            jax.ShapeDtypeStruct((1, blocks), jnp.int32),
            jax.ShapeDtypeStruct((blocks, 1), jnp.int32),
        ],
        in_specs=[scalar, vmem, vmem],
        out_specs=[vmem] * 4,
        cost_estimate=cost(COSTS[6]),
        compiler_params=pltpu.CompilerParams(vmem_limit_bytes=8 << 20),
        name="places",
    )(req_scalar, block_slot[None, :], cache_len.reshape(sources, row_count))

    def pairs(cache):
        cache = cache.reshape(blocks, groups, HD, 2 * HD).transpose(0, 2, 1, 3)
        return cache.reshape(blocks, HD * groups, 2 * HD)

    partial = attend(
        heads, groups, CHUNK, width, query_row, left, slot, local,
        queries, pairs(k_cache), pairs(v_cache),
    )
    parts = send_rows(partial, "req")
    kv_scalar = jnp.reshape(kv_index, (1,)).astype(jnp.int32)
    token_count = row_count // kv_size
    projected = pl.pallas_call(
        functools.partial(merge_kernel, heads, groups, kv_size),
        out_shape=[jax.ShapeDtypeStruct((token_count, model), BF)] * kv_size,
        in_specs=[scalar] + [vmem] * (4 + sources),
        out_specs=[vmem] * kv_size,
        scratch_shapes=[pltpu.VMEM((row_count, model), F32)],
        compiler_params=pltpu.CompilerParams(vmem_limit_bytes=10 << 20),
        cost_estimate=cost(COSTS[3]),
        name="merge",
    )(kv_scalar, query, key_new, value_new, w_out, *parts)
    pieces = [projected[0]]
    for distance in range(1, kv_size):
        pieces.append(swap(projected[distance], "kv", distance))
    after_attn, outgoing = pl.pallas_call(
        route_kernel,
        out_shape=[
            jax.ShapeDtypeStruct((token_count, model), F32),
            jax.ShapeDtypeStruct((token_count, model + 128), BF),
        ],
        in_specs=[scalar] + [vmem] * (4 + kv_size),
        out_specs=[vmem, vmem],
        compiler_params=pltpu.CompilerParams(vmem_limit_bytes=10 << 20),
        cost_estimate=cost(COSTS[4]),
        name="route",
    )(kv_scalar, hidden_in, moe_gain.reshape(-1, 128), w_router, routes, *pieces)
    arrived = gather_rows(outgoing, "req")
    local_experts = w_gate_up.shape[0]
    if STAGE:
        w_gate_up = pl.pallas_call(
            stage_kernel,
            out_shape=jax.ShapeDtypeStruct(w_gate_up.shape, BF),
            in_specs=[pl.BlockSpec(memory_space=pl.ANY), far],
            out_specs=pl.BlockSpec(memory_space=pl.ANY),
            scratch_shapes=[pltpu.SemaphoreType.DMA],
            cost_estimate=cost(2.0),
            compiler_params=pltpu.CompilerParams(vmem_limit_bytes=SLIM << 20),
            name="stage",
        )(outgoing, w_gate_up)
    mixed = pl.pallas_call(
        functools.partial(expert_kernel, sources, w_router.shape[1]),
        grid=(local_experts,),
        out_shape=[jax.ShapeDtypeStruct((token_count, model), BF)] * sources,
        in_specs=[scalar]
        + [vmem] * sources
        + [
            pl.BlockSpec((1,) + w_gate_up.shape[1:], lambda i: (i, 0, 0)),
            pl.BlockSpec((1,) + w_down.shape[1:], lambda i: (i, 0, 0)),
        ],
        out_specs=[vmem] * sources,
        scratch_shapes=[
            pltpu.VMEM((sources * token_count, model + 128), BF),
            pltpu.VMEM((sources * token_count, model), F32),
        ],
        compiler_params=pltpu.CompilerParams(vmem_limit_bytes=24 << 20),
        cost_estimate=cost(COSTS[5]),
        name="experts",
    )(req_scalar, *arrived, w_gate_up, w_down)
    mixture = sum_rows(mixed, "req")
    return (after_attn + mixture).astype(BF)


def solution(mesh):
    placed = (
        P("req", None),
        P(),
        P("kv", None),
        P("kv", None),
        P("kv", None),
        P("kv", None),
        P("req", "kv", None),
        P("req", "kv", None),
        P(),
        P("req"),
        P(),
        P(),
        P("req", None, None),
        P("req", None, None),
        P(("req", "kv"), None),
    )
    return jax.shard_map(
        shards, mesh=mesh, in_specs=placed, out_specs=P(("req", "kv"), None), check_vma=False
    )
```

```python
import functools
import math

import jax
import jax.numpy as jnp
from jax import lax
from jax.experimental import pallas as pl
from jax.experimental.pallas import tpu as pltpu
from jax.sharding import PartitionSpec as P

HD = 64
FFE = 512
BLK = 128
PAGES = 3
CHUNK = 96
QLIM = 60
ALIM = 24
SLIM = 1
STAGE = True
COSTS = (12.0, 1.0, 12.0, 12.0, 12.0, 4.0, 12.0)
NEG = -1e30
BF = jnp.bfloat16
F32 = jnp.float32


def iota(shape, dim):
    return lax.broadcasted_iota(jnp.int32, shape, dim)


def swap(value, axis, distance):
    size = lax.axis_size(axis)
    return lax.ppermute(value, axis, [(source, source ^ distance) for source in range(size)])


def gather_rows(value, axis):
    size = lax.axis_size(axis)
    held = {0: value}
    far = size // 2
    for distance in list(range(far, size, 2)) + list(range(2, far, 2)) + list(range(1, far, 2)):
        held[distance] = swap(value, axis, distance)
    for distance in range(far + 1, size, 2):
        held[distance] = swap(held[distance - 1], axis, 1)
    return [held[distance] for distance in range(size)]


def send_rows(values, axis):
    size = lax.axis_size(axis)
    held = {0: values[0]}
    far = size // 2
    for start in list(range(size - 2, far - 1, -2)) + list(range(2, far, 2)) + [0]:
        for distance in (start, start + 1):
            if distance:
                held[distance] = swap(values[distance], axis, distance)
    return [held[distance] for distance in sorted(held, key=lambda distance: -distance)]


def sum_rows(values, near, axis):
    size = lax.axis_size(axis)
    far = size // 2
    split = far
    count = values[0].shape[0]
    beside = {distance: swap(values[distance], axis, 1) for distance in range(split + 1, size, 2)}
    arrived = [swap(values[distance], axis, distance) for distance in range(far, split)]
    near = swap(near, axis, 1)
    for distance in range(split, size, 2):
        joined = values[distance].astype(F32) + beside[distance + 1].astype(F32)
        arrived.append(swap(joined.astype(BF), axis, distance))
    for distance in range(2, far, 2):
        joined = values[distance].astype(F32) + near[distance // 2 * count : (distance // 2 + 1) * count].astype(F32)
        arrived.append(swap(joined.astype(BF), axis, distance))
    total = values[0].astype(F32) + near[:count].astype(F32)
    for value in arrived:
        total = total + value.astype(F32)
    return total


def cost(micros):
    return pl.CostEstimate(flops=int(micros * 1e9), bytes_accessed=int(micros * 3e6), transcendentals=0)


def project_rows(normed, weight):
    return lax.dot_general(normed, weight, (((1,), (1,)), ((), ())), preferred_element_type=F32)


def dot(left, right):
    return jnp.dot(left, right, preferred_element_type=F32)


def rotate(values, cosines, sines):
    width = values.shape[1]
    low = iota((1, 2 * HD), 1) % HD < HD // 2
    pieces = []
    for start in range(0, width, 2 * HD):
        tile = values[:, start : start + 2 * HD]
        short = 2 * HD - tile.shape[1]
        if short:
            tile = jnp.concatenate([tile, tile], 1)
        turned = jnp.where(low, pltpu.roll(tile, 2 * HD - HD // 2, 1), pltpu.roll(tile, HD // 2, 1))
        pieces.append((tile * cosines + turned * sines)[:, : 2 * HD - short])
    return pieces[0] if len(pieces) == 1 else jnp.concatenate(pieces, 1)


def tables(req_ref, length_ref, rows):
    lengths = jnp.broadcast_to(length_ref[pl.ds(req_ref[0], 1), :].astype(F32), (rows, rows))
    lengths = jnp.where(iota((rows, rows), 0) == iota((rows, rows), 1), lengths, 0.0)
    exponent = (iota((1, 2 * HD), 1) % (HD // 2)).astype(F32) * (-2.0 / HD)
    angles = jnp.sum(lengths, -1, keepdims=True) * jnp.exp(exponent * math.log(10000.0))
    sines = jnp.sin(angles)
    return jnp.cos(angles), jnp.where(iota((1, 2 * HD), 1) % HD < HD // 2, -sines, sines)


def query_kernel(req_ref, hidden_hbm, gain_hbm, weight_hbm, length_hbm, query_ref, hidden_ref, gain_ref, weight_ref,
                 length_ref, sem):
    copies = [
        pltpu.make_async_copy(source, target, sem.at[place])
        for place, (source, target) in enumerate(
            [(length_hbm, length_ref), (hidden_hbm, hidden_ref), (weight_hbm, weight_ref), (gain_hbm, gain_ref)]
        )
    ]
    for copy in copies:
        copy.start()
    copies[0].wait()
    cosines, sines = tables(req_ref, length_ref, query_ref.shape[0])
    copies[1].wait()
    copies[3].wait()
    normed = rms_norm(hidden_ref[...], lanes_of(gain_ref))
    copies[2].wait()
    query = project_rows(normed, weight_ref[...])
    query_ref[...] = (rotate(query, cosines, sines) * 0.125).astype(BF)


def rms_norm(hidden, gain):
    hidden = hidden.astype(F32)
    scale = lax.rsqrt(jnp.mean(hidden * hidden, -1, keepdims=True) + 1e-05)
    return (hidden * scale * gain).astype(BF)


def place_kernel(rows, share, req_ref, block_ref, length_ref, query_ref, left_ref, slot_ref, local_ref):
    blocks = block_ref.shape[1]
    here = iota((blocks, blocks), 0)
    there = iota((blocks, blocks), 1)
    by_lane = block_ref[...]
    by_row = jnp.sum(jnp.where(here == there, by_lane, 0), 1, keepdims=True)
    owner = by_row // PAGES
    home = owner // rows
    local_ref[...] = owner % rows
    query_ref[...] = jnp.bitwise_xor(home, req_ref[0]) * rows + owner % rows
    lengths = lanes_of(length_ref)
    owned = owner == iota((blocks, lengths.shape[1]), 1)
    left = jnp.sum(jnp.where(owned, lengths, 0), 1, keepdims=True) - (by_row - owner * PAGES) * BLK
    left_ref[...] = jnp.sum(jnp.where(here == there, left, 0), 0, keepdims=True)
    lane_home = by_lane // PAGES // rows
    earlier = jnp.logical_and(home == lane_home, here < there)
    rank = jnp.sum(earlier.astype(jnp.int32), 0, keepdims=True)
    slot_ref[...] = jnp.bitwise_xor(lane_home, req_ref[0]) * share + rank


def lanes_of(ref):
    return jnp.concatenate([ref[row : row + 1, :] for row in range(ref.shape[0])], 1)


def fresh_kernel(req_ref, hidden_ref, gain_ref, key_weight_ref, value_weight_ref, length_ref, key_ref, value_ref):
    cosines, sines = tables(req_ref, length_ref, key_ref.shape[0])
    normed = rms_norm(hidden_ref[...], lanes_of(gain_ref))
    key = project_rows(normed, key_weight_ref[...])
    key_ref[...] = rotate(key, cosines, sines).astype(BF)
    value_ref[...] = project_rows(normed, value_weight_ref[...]).astype(BF)


def side_by_side(pairs):
    none = jnp.zeros_like(pairs[:, 0])
    first = jnp.concatenate([pairs[:, 0], none], 2)
    return jnp.concatenate([first, jnp.concatenate([none, pairs[:, 1]], 2)], 1)


def attend_kernel(heads, groups, chunk, nq, *refs):
    qrow_ref, left_ref, slot_ref, local_ref = refs[:4]
    query_refs = refs[4:4+nq]
    key_ref, value_ref = refs[4 + nq : 6 + nq]
    out_refs = refs[6 + nq : -5]
    asked_ref, laid_ref, mean_ref, level_ref, rows_ref = refs[-5:]
    blocks = qrow_ref.shape[0]
    lanes = key_ref.shape[1]
    share, width = out_refs[0].shape
    per_group = heads // groups
    feature = heads * HD
    index = pl.program_id(0)

    @pl.when(index == 0)
    def _():
        queries = jnp.concatenate([query_ref[...] for query_ref in query_refs], 0)
        picked = (iota((blocks, queries.shape[0]), 1) == qrow_ref[...]).astype(BF)
        asked_ref[...] = dot(picked, queries)
        laid_ref[...] = jnp.zeros(laid_ref.shape, F32)

    base = pl.multiple_of(index * chunk, chunk)
    rows = pl.ds(base, chunk)
    low = iota((chunk, 2 * HD), 1) < HD
    for pair in range((heads + 1) // 2):
        stop = min(feature, (pair + 1) * 2 * HD)
        tile = asked_ref[rows, pair * 2 * HD : stop]
        if tile.shape[1] < 2 * HD:
            tile = jnp.concatenate([tile, tile], 1)
        turned = pltpu.roll(tile, HD, 1)
        for odd in range(2):
            head = 2 * pair + odd
            if head < heads:
                first, second = (turned, tile) if odd else (tile, turned)
                laid_ref[pl.ds(head, chunk, 16), :] = jnp.where(low, first, 0.0)
                laid_ref[pl.ds(head + 8, chunk, 16), :] = jnp.where(low, 0.0, second)
    query = laid_ref[: chunk * 16, :].astype(BF)
    query = side_by_side(query.reshape(chunk // 2, 2, 16, 2 * HD)).reshape(chunk // 4, 64, 4 * HD)
    keys = key_ref[...].reshape(chunk // 4, 2, 2, lanes, 2 * HD)
    keys = jnp.concatenate([keys[:, :, 0], keys[:, :, 1]], 3).reshape(chunk // 4, 2 * lanes, 4 * HD)
    scores = lax.dot_general(query, keys, (((2,), (2,)), ((0,), (0,))), preferred_element_type=F32)
    scores = jnp.concatenate([scores[:, None, :32, :lanes], scores[:, None, 32:, lanes:]], 1)
    scores = scores.reshape(chunk, 16, lanes)
    cell_row = iota((8, lanes), 0)
    cell_lane = iota((8, lanes), 1)
    position = jnp.where(cell_lane % groups == cell_row // per_group, 2 * (cell_lane // groups), 1 << 20)
    position = position[None]
    remaining = [jnp.full((1, 8, lanes), left_ref[0, base + place], jnp.int32) for place in range(chunk)]
    remaining = jnp.concatenate(remaining, 0)
    usable = jnp.concatenate([position < remaining, position + 1 < remaining], 1)
    scores = jnp.where(usable, scores, NEG)
    highest = jnp.max(jnp.maximum(scores[:, :8], scores[:, 8:]), -1, keepdims=True)
    weights = jnp.where(usable, jnp.exp(scores - jnp.concatenate([highest, highest], 1)), 0.0)
    total = jnp.sum(weights[:, :8] + weights[:, 8:], -1, keepdims=True)
    weights = side_by_side(weights.astype(BF).reshape(chunk // 2, 2, 16, lanes))
    numer = lax.dot_general(weights, value_ref[...].reshape(chunk // 2, 2 * lanes, 2 * HD), (((2,), (1,)), ((0,), (0,))), preferred_element_type=F32)
    numer = numer.reshape(chunk, 16, 2 * HD)
    numer = jnp.where(iota((1, 8, 2 * HD), 2) < HD, numer[:, :8], numer[:, 8:]).reshape(chunk * 8, 2 * HD)
    numer = numer + pltpu.roll(numer, HD, 1)
    total = total.reshape(chunk * 8, 1)
    highest = highest.reshape(chunk * 8, 1)
    some = total > 0.0
    safe = jnp.where(some, total, 1.0)
    mean_ref[: chunk * 8, :] = numer / safe
    level_ref[: chunk * 8, :] = jnp.broadcast_to(jnp.where(some, highest + jnp.log(safe), NEG), (chunk * 8, 2 * HD))
    lane = iota((chunk, 2 * HD), 1)
    means = [mean_ref[pl.ds(head, chunk, 8), :] for head in range(heads)]
    extras = jnp.zeros((chunk, 2 * HD), F32)
    start = feature % (2 * HD)
    for head in range(heads):
        level = level_ref[pl.ds(head, chunk, 8), :]
        first = level.astype(BF).astype(F32)
        second = (level - first).astype(BF).astype(F32)
        third = level - first - second
        for part, piece in enumerate((first, second, third)):
            extras = jnp.where(lane == start + 4 * head + part, piece, extras)
    extras = jnp.where(lane == start + HD - 1, local_ref[...].astype(F32), extras)
    for pair in range(width // (2 * HD)):
        left = means[2 * pair] if 2 * pair < heads else extras
        right = means[2 * pair + 1] if 2 * pair + 1 < heads else extras
        rows_ref[rows, pair * 2 * HD : (pair + 1) * 2 * HD] = jnp.where(low, left, right).astype(BF)

    @pl.when(index == blocks // chunk - 1)
    def _():
        order = (slot_ref[...] == iota((blocks, blocks), 0)).astype(BF)
        sorted_rows = dot(order, rows_ref[...])
        for place, out_ref in enumerate(out_refs):
            out_ref[...] = sorted_rows[place * share : (place + 1) * share].astype(BF)

def attend(heads, groups, chunk, width, qrow, left, slot, local, queries, keys, values, limit=ALIM):
    blocks, lanes = keys.shape[:2]
    whole = pl.BlockSpec(memory_space=pltpu.VMEM)
    block = lambda *shape: pl.BlockSpec(shape, lambda i: (i,) + (0,) * (len(shape) - 1))
    return pl.pallas_call(
        functools.partial(attend_kernel, heads, groups, chunk, len(queries)),
        grid=(blocks // chunk,),
        out_shape=[jax.ShapeDtypeStruct((blocks // len(queries), width), BF)] * len(queries),
        in_specs=[whole, pl.BlockSpec(memory_space=pltpu.SMEM), whole, block(chunk, 1)] + [whole] * len(queries)
        + [block(chunk, lanes, 2 * HD)] * 2,
        out_specs=[whole] * len(queries),
        scratch_shapes=[
            pltpu.VMEM((blocks, heads * HD), F32),
            pltpu.VMEM((chunk * 16 + 16, 2 * HD), F32),
            pltpu.VMEM((chunk * 8 + 8, 2 * HD), F32),
            pltpu.VMEM((chunk * 8 + 8, 2 * HD), F32),
            pltpu.VMEM((blocks, width), BF),
        ],
        compiler_params=pltpu.CompilerParams(vmem_limit_bytes=limit << 20),
        cost_estimate=cost(COSTS[2]),
        name="attend",
    )(qrow, left, slot, local, *queries, keys, values)


def merge_kernel(heads, groups, tokens, *refs):
    kv_ref, query_ref, key_ref, value_ref, weight_ref = refs[:5]
    keep_refs = refs[-2 - tokens // 2 : -2]
    give_ref, result_ref = refs[-2:]
    part_refs = refs[5 : -2 - tokens // 2]
    parts = jnp.concatenate([part_ref[...] for part_ref in part_refs], 0)
    rows = query_ref.shape[0]
    blocks, width = parts.shape
    per_group = heads // groups
    feature = heads * HD
    row = iota((32, width), 0)
    column = iota((32, width), 1) - feature
    wanted = jnp.where(row < 24, (row % 8) * 4 + row // 8, HD - 1)
    pick = jnp.logical_and(column == wanted, jnp.logical_or(row == 24, row % 8 < heads))
    pick = jnp.logical_and(pick, row <= 24).astype(BF)
    extras = lax.dot_general(pick, parts, (((1,), (1,)), ((), ())), preferred_element_type=F32)
    levels = extras[0:8] + extras[8:16] + extras[16:24]
    local = extras[24:25].astype(jnp.int32)
    member = local == iota((rows, blocks), 0)

    source = iota((groups * HD, width), 0)
    target = iota((groups * HD, width), 1)
    same = jnp.logical_and(source // HD == target // (HD * per_group), source % HD == target % HD)
    widen = same.astype(BF)
    key = dot(key_ref[...], widen)
    value = dot(value_ref[...], widen)
    products = query_ref[...].astype(F32) * key[:, :feature]
    lane_head = iota((rows, width), 1) // HD
    joined = jnp.zeros((rows, width), F32)
    for head in range(heads):
        own = jnp.sum(jnp.where(lane_head[:, :feature] == head, products, 0.0), -1, keepdims=True)
        level = levels[head : head + 1]
        highest = jnp.max(jnp.where(member, level, NEG), -1, keepdims=True)
        highest = jnp.maximum(highest, own)
        weights = jnp.where(member, jnp.exp(level - highest), 0.0).astype(BF)
        own_weight = jnp.exp(own - highest)
        total = jnp.sum(weights.astype(F32), -1, keepdims=True) + own_weight
        numer = dot(weights, parts) + own_weight * value
        joined = jnp.where(lane_head == head, numer / total, joined)
    attended = joined[:, :feature].astype(BF)
    result_ref[...] = dot(attended, weight_ref[...])
    count = rows // tokens
    for place in range(tokens):
        start = pl.multiple_of(jnp.bitwise_xor(kv_ref[0], place) * count, count)
        piece = result_ref[pl.ds(start, count), :].astype(BF)
        if place % 2:
            give_ref[place // 2 * count : (place // 2 + 1) * count, :] = piece
        else:
            keep_refs[place // 2][...] = piece


def route_kernel(kv_ref, hidden_ref, gain_ref, router_ref, routes_ref, given_ref, *refs):
    piece_refs = refs[:-2]
    after_ref, out_ref = refs[-2:]
    count, model = after_ref.shape
    start = pl.multiple_of(kv_ref[0] * count, count)
    total = given_ref[:count, :].astype(F32)
    for piece_ref in piece_refs:
        total = total + piece_ref[...].astype(F32)
    after = hidden_ref[pl.ds(start, count), :].astype(F32) + total
    after_ref[...] = after
    scale = lax.rsqrt(jnp.mean(after * after, -1, keepdims=True) + 1e-05)
    normed = (after * scale * lanes_of(gain_ref)).astype(BF)
    out_ref[:, :model] = normed
    experts = router_ref.shape[1]
    logits = dot(normed, router_ref[...])
    expert = iota((count, experts), 1)
    chosen = expert == routes_ref[:, 0:1]
    for turn in range(1, routes_ref.shape[1]):
        chosen = jnp.logical_or(chosen, expert == routes_ref[:, turn : turn + 1])
    logits = jnp.where(chosen, logits, NEG)
    gates = jnp.where(chosen, jnp.exp(logits - jnp.max(logits, -1, keepdims=True)), 0.0)
    gates = gates / jnp.sum(gates, -1, keepdims=True)
    high = gates.astype(BF).astype(F32)
    spare = jnp.zeros((count, 128 - 2 * experts), F32)
    out_ref[:, model:] = jnp.concatenate([high, gates - high, spare], 1).astype(BF)


def stage_kernel(order_ref, source_ref, target_ref, sem):
    copy = pltpu.make_async_copy(source_ref, target_ref, sem)
    copy.start()
    copy.wait()


def expert_kernel(sources, experts, req_ref, *refs):
    token_refs = refs[:sources]
    up_ref, down_ref = refs[sources : sources + 2]
    out_refs = refs[sources + 2 : -2]
    tokens_ref, mixed_ref = refs[-2:]
    index = pl.program_id(0)
    count, model = out_refs[0].shape
    hidden = down_ref.shape[1]

    @pl.when(index == 0)
    def _():
        for place, token_ref in enumerate(token_refs):
            tokens_ref[place * count : (place + 1) * count, :] = token_ref[...]

    lane = iota((sources * count, 128), 1)
    mine = req_ref[0] * pl.num_programs(0) + index
    gates = tokens_ref[:, model:].astype(F32)
    picked = jnp.logical_or(lane == mine, lane == mine + experts)
    gate = jnp.sum(jnp.where(picked, gates, 0.0), -1, keepdims=True)
    both = dot(tokens_ref[:, :model], up_ref[0])
    active = (jax.nn.silu(both[:, :hidden]) * both[:, hidden:]).astype(BF)
    produced = dot(active, down_ref[0]).astype(BF).astype(F32) * gate

    @pl.when(index == 0)
    def _():
        mixed_ref[...] = produced

    @pl.when(index > 0)
    def _():
        mixed_ref[...] += produced

    @pl.when(index == pl.num_programs(0) - 1)
    def _():
        far = sources // 2
        out_ref = iter(out_refs[:-1])
        for place in range(sources):
            piece = mixed_ref[place * count : (place + 1) * count, :].astype(BF)
            if place < far and place % 2:
                out_refs[-1][place // 2 * count : (place // 2 + 1) * count, :] = piece
            else:
                next(out_ref)[...] = piece


def shards(
    hidden_in,
    attn_gain,
    w_query,
    w_key,
    w_value,
    w_out,
    k_cache,
    v_cache,
    cache_len,
    block_slot,
    moe_gain,
    w_router,
    w_gate_up,
    w_down,
    routes,
):
    req_index = lax.axis_index("req")
    kv_index = lax.axis_index("kv")
    sources = lax.axis_size("req")
    kv_size = lax.axis_size("kv")
    row_count, model = hidden_in.shape
    heads = w_query.shape[0] // HD
    groups = w_key.shape[0] // HD
    blocks = k_cache.shape[0]
    requests = cache_len.shape[0]
    share = blocks // sources
    width = -(-(heads * HD + HD) // 128) * 128

    vmem = pl.BlockSpec(memory_space=pltpu.VMEM)
    scalar = pl.BlockSpec(memory_space=pltpu.SMEM)
    req_scalar = jnp.reshape(req_index, (1,)).astype(jnp.int32)
    far = pl.BlockSpec(memory_space=pltpu.HBM)
    gain = attn_gain.reshape(-1, 128)
    lengths = cache_len.reshape(sources, row_count)
    query = pl.pallas_call(
        query_kernel,
        out_shape=jax.ShapeDtypeStruct((row_count, heads * HD), BF),
        in_specs=[scalar] + [far] * 4,
        out_specs=vmem,
        scratch_shapes=[
            pltpu.VMEM((row_count, model), BF),
            pltpu.VMEM((model // 128, 128), F32),
            pltpu.VMEM(w_query.shape, BF),
            pltpu.VMEM((sources, row_count), jnp.int32),
            pltpu.SemaphoreType.DMA((4,)),
        ],
        cost_estimate=cost(COSTS[0]),
        compiler_params=pltpu.CompilerParams(vmem_limit_bytes=QLIM << 20),
        name="query",
    )(req_scalar, hidden_in, gain, w_query, lengths)
    key_new, value_new = pl.pallas_call(
        fresh_kernel,
        out_shape=[jax.ShapeDtypeStruct((row_count, groups * HD), BF)] * 2,
        in_specs=[scalar] + [vmem] * 5,
        out_specs=[vmem] * 2,
        cost_estimate=cost(COSTS[1]),
        compiler_params=pltpu.CompilerParams(vmem_limit_bytes=8 << 20),
        name="fresh",
    )(req_scalar, hidden_in, gain, w_key, w_value, lengths)
    queries = gather_rows(query, "req")

    query_row, left, slot, local = pl.pallas_call(
        functools.partial(place_kernel, row_count, share),
        out_shape=[
            jax.ShapeDtypeStruct((blocks, 1), jnp.int32),
            jax.ShapeDtypeStruct((1, blocks), jnp.int32),
            jax.ShapeDtypeStruct((1, blocks), jnp.int32),
            jax.ShapeDtypeStruct((blocks, 1), jnp.int32),
        ],
        in_specs=[scalar, vmem, vmem],
        out_specs=[vmem] * 4,
        cost_estimate=cost(COSTS[6]),
        compiler_params=pltpu.CompilerParams(vmem_limit_bytes=8 << 20),
        name="places",
    )(req_scalar, block_slot[None, :], lengths)

    def pairs(cache):
        cache = cache.reshape(blocks, groups, HD, 2 * HD).transpose(0, 2, 1, 3)
        return cache.reshape(blocks, HD * groups, 2 * HD)

    partial = attend(
        heads, groups, CHUNK, width, query_row, left, slot, local,
        queries, pairs(k_cache), pairs(v_cache),
    )
    parts = send_rows(partial, "req")
    kv_scalar = jnp.reshape(kv_index, (1,)).astype(jnp.int32)
    token_count = row_count // kv_size
    projected = pl.pallas_call(
        functools.partial(merge_kernel, heads, groups, kv_size),
        out_shape=[jax.ShapeDtypeStruct((token_count, model), BF)] * (kv_size // 2)
        + [jax.ShapeDtypeStruct((kv_size // 2 * token_count, model), BF)],
        in_specs=[scalar] + [vmem] * (4 + sources),
        out_specs=[vmem] * (kv_size // 2 + 1),
        scratch_shapes=[pltpu.VMEM((row_count, model), F32)],
        compiler_params=pltpu.CompilerParams(vmem_limit_bytes=10 << 20),
        cost_estimate=cost(COSTS[3]),
        name="merge",
    )(kv_scalar, query, key_new, value_new, w_out, *parts)
    given = swap(projected[-1], "kv", 1)
    pieces = [projected[0]]
    for place in range(1, kv_size // 2):
        joined = given[place * token_count : (place + 1) * token_count].astype(F32)
        joined = (projected[place].astype(F32) + joined).astype(BF)
        pieces.append(swap(joined, "kv", 2 * place))
    after_attn, outgoing = pl.pallas_call(
        route_kernel,
        out_shape=[
            jax.ShapeDtypeStruct((token_count, model), F32),
            jax.ShapeDtypeStruct((token_count, model + 128), BF),
        ],
        in_specs=[scalar] + [vmem] * (5 + kv_size // 2),
        out_specs=[vmem, vmem],
        compiler_params=pltpu.CompilerParams(vmem_limit_bytes=10 << 20),
        cost_estimate=cost(COSTS[4]),
        name="route",
    )(kv_scalar, hidden_in, moe_gain.reshape(-1, 128), w_router, routes, given, *pieces)
    arrived = gather_rows(outgoing, "req")
    local_experts = w_gate_up.shape[0]
    if STAGE:
        w_gate_up = pl.pallas_call(
            stage_kernel,
            out_shape=jax.ShapeDtypeStruct(w_gate_up.shape, BF),
            in_specs=[pl.BlockSpec(memory_space=pl.ANY), far],
            out_specs=pl.BlockSpec(memory_space=pl.ANY),
            scratch_shapes=[pltpu.SemaphoreType.DMA],
            cost_estimate=cost(2.0),
            compiler_params=pltpu.CompilerParams(vmem_limit_bytes=SLIM << 20),
            name="stage",
        )(outgoing, w_gate_up)
    single = [distance for distance in range(sources) if distance % 2 == 0 or distance > sources // 2]
    mixed = pl.pallas_call(
        functools.partial(expert_kernel, sources, w_router.shape[1]),
        grid=(local_experts,),
        out_shape=[jax.ShapeDtypeStruct((token_count, model), BF)] * len(single)
        + [jax.ShapeDtypeStruct((sources // 4 * token_count, model), BF)],
        in_specs=[scalar]
        + [vmem] * sources
        + [
            pl.BlockSpec((1,) + w_gate_up.shape[1:], lambda i: (i, 0, 0)),
            pl.BlockSpec((1,) + w_down.shape[1:], lambda i: (i, 0, 0)),
        ],
        out_specs=[vmem] * (len(single) + 1),
        scratch_shapes=[
            pltpu.VMEM((sources * token_count, model + 128), BF),
            pltpu.VMEM((sources * token_count, model), F32),
        ],
        compiler_params=pltpu.CompilerParams(vmem_limit_bytes=24 << 20),
        cost_estimate=cost(COSTS[5]),
        name="experts",
    )(req_scalar, *arrived, w_gate_up, w_down)
    mixture = sum_rows(dict(zip(single, mixed)), mixed[-1], "req")
    return (after_attn + mixture).astype(BF)


def solution(mesh):
    placed = (
        P("req", None),
        P(),
        P("kv", None),
        P("kv", None),
        P("kv", None),
        P("kv", None),
        P("req", "kv", None),
        P("req", "kv", None),
        P(),
        P("req"),
        P(),
        P(),
        P("req", None, None),
        P("req", None, None),
        P(("req", "kv"), None),
    )
    return jax.shard_map(
        shards, mesh=mesh, in_specs=placed, out_specs=P(("req", "kv"), None), check_vma=False
    )
```

```python
import functools
import math

import jax
import jax.numpy as jnp
from jax import lax
from jax.experimental import pallas as pl
from jax.experimental.pallas import tpu as pltpu
from jax.sharding import PartitionSpec as P

HD = 64
FFE = 512
BLK = 128
PAGES = 3
CHUNK = 96
QLIM = 60
ALIM = 24
SLIM = 1
STAGE = True
COSTS = (12.0, 1.0, 12.0, 12.0, 12.0, 4.0, 12.0)
NEG = -1e30
BF = jnp.bfloat16
F32 = jnp.float32


def iota(shape, dim):
    return lax.broadcasted_iota(jnp.int32, shape, dim)


def swap(value, axis, distance):
    size = lax.axis_size(axis)
    return lax.ppermute(value, axis, [(source, source ^ distance) for source in range(size)])


def gather_rows(value, axis):
    size = lax.axis_size(axis)
    far = size // 2
    held = {0: value, far: swap(value, axis, far)}
    for distance in range(far - 1, 0, -1):
        held[distance] = swap(value, axis, distance)
    for distance in range(far - 1, 0, -1):
        held[far + distance] = swap(held[far], axis, distance)
    return [held[distance] for distance in range(size)]


def send_rows(values, axis):
    size = lax.axis_size(axis)
    held = {0: values[0]}
    far = size // 2
    for start in list(range(size - 2, far - 1, -2)) + list(range(2, far, 2)) + [0]:
        for distance in (start, start + 1):
            if distance:
                held[distance] = swap(values[distance], axis, distance)
    return [held[distance] for distance in sorted(held, key=lambda distance: -distance)]


def sum_rows(values, axis):
    size = lax.axis_size(axis)
    far = size // 2
    beside = [swap(values[far + distance], axis, distance) for distance in range(far - 1, 0, -1)]
    joined = values[far].astype(F32)
    for value in beside:
        joined = joined + value.astype(F32)
    joined, near = joined.astype(BF), values[1:far]
    arrived = [swap(joined, axis, far)]
    arrived += [swap(near[distance - 1], axis, distance) for distance in range(far - 1, 0, -1)]
    total = values[0].astype(F32)
    for value in arrived:
        total = total + value.astype(F32)
    return total


def cost(micros):
    return pl.CostEstimate(flops=int(micros * 1e9), bytes_accessed=int(micros * 3e6), transcendentals=0)


def project_rows(normed, weight):
    return lax.dot_general(normed, weight, (((1,), (1,)), ((), ())), preferred_element_type=F32)


def dot(left, right):
    return jnp.dot(left, right, preferred_element_type=F32)


def rotate(values, cosines, sines):
    width = values.shape[1]
    low = iota((1, 2 * HD), 1) % HD < HD // 2
    pieces = []
    for start in range(0, width, 2 * HD):
        tile = values[:, start : start + 2 * HD]
        short = 2 * HD - tile.shape[1]
        if short:
            tile = jnp.concatenate([tile, tile], 1)
        turned = jnp.where(low, pltpu.roll(tile, 2 * HD - HD // 2, 1), pltpu.roll(tile, HD // 2, 1))
        pieces.append((tile * cosines + turned * sines)[:, : 2 * HD - short])
    return pieces[0] if len(pieces) == 1 else jnp.concatenate(pieces, 1)


def tables(req_ref, length_ref, rows):
    lengths = jnp.broadcast_to(length_ref[pl.ds(req_ref[0], 1), :].astype(F32), (rows, rows))
    lengths = jnp.where(iota((rows, rows), 0) == iota((rows, rows), 1), lengths, 0.0)
    exponent = (iota((1, 2 * HD), 1) % (HD // 2)).astype(F32) * (-2.0 / HD)
    angles = jnp.sum(lengths, -1, keepdims=True) * jnp.exp(exponent * math.log(10000.0))
    sines = jnp.sin(angles)
    return jnp.cos(angles), jnp.where(iota((1, 2 * HD), 1) % HD < HD // 2, -sines, sines)


def query_kernel(req_ref, hidden_hbm, gain_hbm, weight_hbm, length_hbm, query_ref, hidden_ref, gain_ref, weight_ref,
                 length_ref, sem):
    copies = [
        pltpu.make_async_copy(source, target, sem.at[place])
        for place, (source, target) in enumerate(
            [(length_hbm, length_ref), (hidden_hbm, hidden_ref), (weight_hbm, weight_ref), (gain_hbm, gain_ref)]
        )
    ]
    for copy in copies:
        copy.start()
    copies[0].wait()
    cosines, sines = tables(req_ref, length_ref, query_ref.shape[0])
    copies[1].wait()
    copies[3].wait()
    normed = rms_norm(hidden_ref[...], lanes_of(gain_ref))
    copies[2].wait()
    query = project_rows(normed, weight_ref[...])
    query_ref[...] = (rotate(query, cosines, sines) * 0.125).astype(BF)


def rms_norm(hidden, gain):
    hidden = hidden.astype(F32)
    scale = lax.rsqrt(jnp.mean(hidden * hidden, -1, keepdims=True) + 1e-05)
    return (hidden * scale * gain).astype(BF)


def place_kernel(rows, share, req_ref, block_ref, length_ref, query_ref, left_ref, slot_ref, local_ref):
    blocks = block_ref.shape[1]
    here = iota((blocks, blocks), 0)
    there = iota((blocks, blocks), 1)
    by_lane = block_ref[...]
    by_row = jnp.sum(jnp.where(here == there, by_lane, 0), 1, keepdims=True)
    owner = by_row // PAGES
    home = owner // rows
    local_ref[...] = owner % rows
    query_ref[...] = jnp.bitwise_xor(home, req_ref[0]) * rows + owner % rows
    lengths = lanes_of(length_ref)
    owned = owner == iota((blocks, lengths.shape[1]), 1)
    left = jnp.sum(jnp.where(owned, lengths, 0), 1, keepdims=True) - (by_row - owner * PAGES) * BLK
    left_ref[...] = jnp.sum(jnp.where(here == there, left, 0), 0, keepdims=True)
    lane_home = by_lane // PAGES // rows
    earlier = jnp.logical_and(home == lane_home, here < there)
    rank = jnp.sum(earlier.astype(jnp.int32), 0, keepdims=True)
    slot_ref[...] = jnp.bitwise_xor(lane_home, req_ref[0]) * share + rank


def lanes_of(ref):
    return jnp.concatenate([ref[row : row + 1, :] for row in range(ref.shape[0])], 1)


def fresh_kernel(req_ref, hidden_ref, gain_ref, key_weight_ref, value_weight_ref, length_ref, key_ref, value_ref):
    cosines, sines = tables(req_ref, length_ref, key_ref.shape[0])
    normed = rms_norm(hidden_ref[...], lanes_of(gain_ref))
    key = project_rows(normed, key_weight_ref[...])
    key_ref[...] = rotate(key, cosines, sines).astype(BF)
    value_ref[...] = project_rows(normed, value_weight_ref[...]).astype(BF)


def side_by_side(pairs):
    none = jnp.zeros_like(pairs[:, 0])
    first = jnp.concatenate([pairs[:, 0], none], 2)
    return jnp.concatenate([first, jnp.concatenate([none, pairs[:, 1]], 2)], 1)


def attend_kernel(heads, groups, chunk, nq, *refs):
    qrow_ref, left_ref, slot_ref, local_ref = refs[:4]
    query_refs = refs[4:4+nq]
    key_ref, value_ref = refs[4 + nq : 6 + nq]
    out_refs = refs[6 + nq : -5]
    asked_ref, laid_ref, mean_ref, level_ref, rows_ref = refs[-5:]
    blocks = qrow_ref.shape[0]
    lanes = key_ref.shape[1]
    share, width = out_refs[0].shape
    per_group = heads // groups
    feature = heads * HD
    index = pl.program_id(0)

    @pl.when(index == 0)
    def _():
        queries = jnp.concatenate([query_ref[...] for query_ref in query_refs], 0)
        picked = (iota((blocks, queries.shape[0]), 1) == qrow_ref[...]).astype(BF)
        asked_ref[...] = dot(picked, queries)
        laid_ref[...] = jnp.zeros(laid_ref.shape, F32)

    base = pl.multiple_of(index * chunk, chunk)
    rows = pl.ds(base, chunk)
    low = iota((chunk, 2 * HD), 1) < HD
    for pair in range((heads + 1) // 2):
        stop = min(feature, (pair + 1) * 2 * HD)
        tile = asked_ref[rows, pair * 2 * HD : stop]
        if tile.shape[1] < 2 * HD:
            tile = jnp.concatenate([tile, tile], 1)
        turned = pltpu.roll(tile, HD, 1)
        for odd in range(2):
            head = 2 * pair + odd
            if head < heads:
                first, second = (turned, tile) if odd else (tile, turned)
                laid_ref[pl.ds(head, chunk, 16), :] = jnp.where(low, first, 0.0)
                laid_ref[pl.ds(head + 8, chunk, 16), :] = jnp.where(low, 0.0, second)
    query = laid_ref[: chunk * 16, :].astype(BF)
    query = side_by_side(query.reshape(chunk // 2, 2, 16, 2 * HD)).reshape(chunk // 4, 64, 4 * HD)
    keys = key_ref[...].reshape(chunk // 4, 2, 2, lanes, 2 * HD)
    keys = jnp.concatenate([keys[:, :, 0], keys[:, :, 1]], 3).reshape(chunk // 4, 2 * lanes, 4 * HD)
    scores = lax.dot_general(query, keys, (((2,), (2,)), ((0,), (0,))), preferred_element_type=F32)
    scores = jnp.concatenate([scores[:, None, :32, :lanes], scores[:, None, 32:, lanes:]], 1)
    scores = scores.reshape(chunk, 16, lanes)
    cell_row = iota((8, lanes), 0)
    cell_lane = iota((8, lanes), 1)
    position = jnp.where(cell_lane % groups == cell_row // per_group, 2 * (cell_lane // groups), 1 << 20)
    position = position[None]
    remaining = [jnp.full((1, 8, lanes), left_ref[0, base + place], jnp.int32) for place in range(chunk)]
    remaining = jnp.concatenate(remaining, 0)
    usable = jnp.concatenate([position < remaining, position + 1 < remaining], 1)
    scores = jnp.where(usable, scores, NEG)
    highest = jnp.max(jnp.maximum(scores[:, :8], scores[:, 8:]), -1, keepdims=True)
    weights = jnp.where(usable, jnp.exp(scores - jnp.concatenate([highest, highest], 1)), 0.0)
    total = jnp.sum(weights[:, :8] + weights[:, 8:], -1, keepdims=True)
    weights = side_by_side(weights.astype(BF).reshape(chunk // 2, 2, 16, lanes))
    numer = lax.dot_general(weights, value_ref[...].reshape(chunk // 2, 2 * lanes, 2 * HD), (((2,), (1,)), ((0,), (0,))), preferred_element_type=F32)
    numer = numer.reshape(chunk, 16, 2 * HD)
    numer = jnp.where(iota((1, 8, 2 * HD), 2) < HD, numer[:, :8], numer[:, 8:]).reshape(chunk * 8, 2 * HD)
    numer = numer + pltpu.roll(numer, HD, 1)
    total = total.reshape(chunk * 8, 1)
    highest = highest.reshape(chunk * 8, 1)
    some = total > 0.0
    safe = jnp.where(some, total, 1.0)
    mean_ref[: chunk * 8, :] = numer / safe
    level_ref[: chunk * 8, :] = jnp.broadcast_to(jnp.where(some, highest + jnp.log(safe), NEG), (chunk * 8, 2 * HD))
    lane = iota((chunk, 2 * HD), 1)
    means = [mean_ref[pl.ds(head, chunk, 8), :] for head in range(heads)]
    extras = jnp.zeros((chunk, 2 * HD), F32)
    start = feature % (2 * HD)
    for head in range(heads):
        level = level_ref[pl.ds(head, chunk, 8), :]
        first = level.astype(BF).astype(F32)
        second = (level - first).astype(BF).astype(F32)
        third = level - first - second
        for part, piece in enumerate((first, second, third)):
            extras = jnp.where(lane == start + 4 * head + part, piece, extras)
    extras = jnp.where(lane == start + HD - 1, local_ref[...].astype(F32), extras)
    for pair in range(width // (2 * HD)):
        left = means[2 * pair] if 2 * pair < heads else extras
        right = means[2 * pair + 1] if 2 * pair + 1 < heads else extras
        rows_ref[rows, pair * 2 * HD : (pair + 1) * 2 * HD] = jnp.where(low, left, right).astype(BF)

    @pl.when(index == blocks // chunk - 1)
    def _():
        order = (slot_ref[...] == iota((blocks, blocks), 0)).astype(BF)
        sorted_rows = dot(order, rows_ref[...])
        for place, out_ref in enumerate(out_refs):
            out_ref[...] = sorted_rows[place * share : (place + 1) * share].astype(BF)

def attend(heads, groups, chunk, width, qrow, left, slot, local, queries, keys, values, limit=ALIM):
    blocks, lanes = keys.shape[:2]
    whole = pl.BlockSpec(memory_space=pltpu.VMEM)
    block = lambda *shape: pl.BlockSpec(shape, lambda i: (i,) + (0,) * (len(shape) - 1))
    return pl.pallas_call(
        functools.partial(attend_kernel, heads, groups, chunk, len(queries)),
        grid=(blocks // chunk,),
        out_shape=[jax.ShapeDtypeStruct((blocks // len(queries), width), BF)] * len(queries),
        in_specs=[whole, pl.BlockSpec(memory_space=pltpu.SMEM), whole, block(chunk, 1)] + [whole] * len(queries)
        + [block(chunk, lanes, 2 * HD)] * 2,
        out_specs=[whole] * len(queries),
        scratch_shapes=[
            pltpu.VMEM((blocks, heads * HD), F32),
            pltpu.VMEM((chunk * 16 + 16, 2 * HD), F32),
            pltpu.VMEM((chunk * 8 + 8, 2 * HD), F32),
            pltpu.VMEM((chunk * 8 + 8, 2 * HD), F32),
            pltpu.VMEM((blocks, width), BF),
        ],
        compiler_params=pltpu.CompilerParams(vmem_limit_bytes=limit << 20),
        cost_estimate=cost(COSTS[2]),
        name="attend",
    )(qrow, left, slot, local, *queries, keys, values)


def merge_kernel(heads, groups, tokens, *refs):
    kv_ref, query_ref, key_ref, value_ref, weight_ref = refs[:5]
    keep_refs = refs[-2 - tokens // 2 : -2]
    give_ref, result_ref = refs[-2:]
    part_refs = refs[5 : -2 - tokens // 2]
    parts = jnp.concatenate([part_ref[...] for part_ref in part_refs], 0)
    rows = query_ref.shape[0]
    blocks, width = parts.shape
    per_group = heads // groups
    feature = heads * HD
    row = iota((32, width), 0)
    column = iota((32, width), 1) - feature
    wanted = jnp.where(row < 24, (row % 8) * 4 + row // 8, HD - 1)
    pick = jnp.logical_and(column == wanted, jnp.logical_or(row == 24, row % 8 < heads))
    pick = jnp.logical_and(pick, row <= 24).astype(BF)
    extras = lax.dot_general(pick, parts, (((1,), (1,)), ((), ())), preferred_element_type=F32)
    levels = extras[0:8] + extras[8:16] + extras[16:24]
    local = extras[24:25].astype(jnp.int32)
    member = local == iota((rows, blocks), 0)

    source = iota((groups * HD, width), 0)
    target = iota((groups * HD, width), 1)
    same = jnp.logical_and(source // HD == target // (HD * per_group), source % HD == target % HD)
    widen = same.astype(BF)
    key = dot(key_ref[...], widen)
    value = dot(value_ref[...], widen)
    products = query_ref[...].astype(F32) * key[:, :feature]
    lane_head = iota((rows, width), 1) // HD
    shares, owns, totals = [], [], []
    for head in range(heads):
        own = jnp.sum(jnp.where(lane_head[:, :feature] == head, products, 0.0), -1, keepdims=True)
        level = levels[head : head + 1]
        highest = jnp.max(jnp.where(member, level, NEG), -1, keepdims=True)
        highest = jnp.maximum(highest, own)
        weights = jnp.where(member, jnp.exp(level - highest), 0.0).astype(BF)
        own_weight = jnp.exp(own - highest)
        shares.append(weights)
        owns.append(own_weight)
        totals.append(jnp.sum(weights.astype(F32), -1, keepdims=True) + own_weight)
    numers = dot(jnp.concatenate(shares, 0), parts)
    joined = jnp.zeros((rows, width), F32)
    for head in range(heads):
        numer = numers[head * rows : (head + 1) * rows] + owns[head] * value
        joined = jnp.where(lane_head == head, numer / totals[head], joined)
    attended = joined[:, :feature].astype(BF)
    result_ref[...] = dot(attended, weight_ref[...])
    count = rows // tokens
    for place in range(tokens):
        start = pl.multiple_of(jnp.bitwise_xor(kv_ref[0], place) * count, count)
        piece = result_ref[pl.ds(start, count), :].astype(BF)
        if place % 2:
            give_ref[place // 2 * count : (place // 2 + 1) * count, :] = piece
        else:
            keep_refs[place // 2][...] = piece


def route_kernel(kv_ref, hidden_ref, gain_ref, router_ref, routes_ref, given_ref, *refs):
    piece_refs = refs[:-2]
    after_ref, out_ref = refs[-2:]
    count, model = after_ref.shape
    start = pl.multiple_of(kv_ref[0] * count, count)
    total = given_ref[:count, :].astype(F32)
    for piece_ref in piece_refs:
        total = total + piece_ref[...].astype(F32)
    after = hidden_ref[pl.ds(start, count), :].astype(F32) + total
    after_ref[...] = after
    scale = lax.rsqrt(jnp.mean(after * after, -1, keepdims=True) + 1e-05)
    normed = (after * scale * lanes_of(gain_ref)).astype(BF)
    out_ref[:, :model] = normed
    experts = router_ref.shape[1]
    logits = dot(normed, router_ref[...])
    expert = iota((count, experts), 1)
    chosen = expert == routes_ref[:, 0:1]
    for turn in range(1, routes_ref.shape[1]):
        chosen = jnp.logical_or(chosen, expert == routes_ref[:, turn : turn + 1])
    logits = jnp.where(chosen, logits, NEG)
    gates = jnp.where(chosen, jnp.exp(logits - jnp.max(logits, -1, keepdims=True)), 0.0)
    gates = gates / jnp.sum(gates, -1, keepdims=True)
    high = gates.astype(BF).astype(F32)
    spare = jnp.zeros((count, 128 - 2 * experts), F32)
    out_ref[:, model:] = jnp.concatenate([high, gates - high, spare], 1).astype(BF)


def stage_kernel(order_ref, source_ref, target_ref, sem):
    copy = pltpu.make_async_copy(source_ref, target_ref, sem)
    copy.start()
    copy.wait()


def expert_kernel(sources, experts, req_ref, *refs):
    token_refs = refs[:sources]
    up_ref, down_ref = refs[sources : sources + 2]
    out_refs = refs[sources + 2 : -2]
    tokens_ref, mixed_ref = refs[-2:]
    index = pl.program_id(0)
    count, model = out_refs[0].shape
    hidden = down_ref.shape[1]

    @pl.when(index == 0)
    def _():
        for place, token_ref in enumerate(token_refs):
            tokens_ref[place * count : (place + 1) * count, :] = token_ref[...]

    lane = iota((sources * count, 128), 1)
    mine = req_ref[0] * pl.num_programs(0) + index
    gates = tokens_ref[:, model:].astype(F32)
    picked = jnp.logical_or(lane == mine, lane == mine + experts)
    gate = jnp.sum(jnp.where(picked, gates, 0.0), -1, keepdims=True)
    both = dot(tokens_ref[:, :model], up_ref[0])
    active = (jax.nn.silu(both[:, :hidden]) * both[:, hidden:]).astype(BF)
    produced = dot(active, down_ref[0]).astype(BF).astype(F32) * gate

    @pl.when(index == 0)
    def _():
        mixed_ref[...] = produced

    @pl.when(index > 0)
    def _():
        mixed_ref[...] += produced

    @pl.when(index == pl.num_programs(0) - 1)
    def _():
        for place, out_ref in enumerate(out_refs):
            out_ref[...] = mixed_ref[place * count : (place + 1) * count, :].astype(BF)


def shards(
    hidden_in,
    attn_gain,
    w_query,
    w_key,
    w_value,
    w_out,
    k_cache,
    v_cache,
    cache_len,
    block_slot,
    moe_gain,
    w_router,
    w_gate_up,
    w_down,
    routes,
):
    req_index = lax.axis_index("req")
    kv_index = lax.axis_index("kv")
    sources = lax.axis_size("req")
    kv_size = lax.axis_size("kv")
    row_count, model = hidden_in.shape
    heads = w_query.shape[0] // HD
    groups = w_key.shape[0] // HD
    blocks = k_cache.shape[0]
    requests = cache_len.shape[0]
    share = blocks // sources
    width = -(-(heads * HD + HD) // 128) * 128

    vmem = pl.BlockSpec(memory_space=pltpu.VMEM)
    scalar = pl.BlockSpec(memory_space=pltpu.SMEM)
    req_scalar = jnp.reshape(req_index, (1,)).astype(jnp.int32)
    far = pl.BlockSpec(memory_space=pltpu.HBM)
    gain = attn_gain.reshape(-1, 128)
    lengths = cache_len.reshape(sources, row_count)
    query = pl.pallas_call(
        query_kernel,
        out_shape=jax.ShapeDtypeStruct((row_count, heads * HD), BF),
        in_specs=[scalar] + [far] * 4,
        out_specs=vmem,
        scratch_shapes=[
            pltpu.VMEM((row_count, model), BF),
            pltpu.VMEM((model // 128, 128), F32),
            pltpu.VMEM(w_query.shape, BF),
            pltpu.VMEM((sources, row_count), jnp.int32),
            pltpu.SemaphoreType.DMA((4,)),
        ],
        cost_estimate=cost(COSTS[0]),
        compiler_params=pltpu.CompilerParams(vmem_limit_bytes=QLIM << 20),
        name="query",
    )(req_scalar, hidden_in, gain, w_query, lengths)
    key_new, value_new = pl.pallas_call(
        fresh_kernel,
        out_shape=[jax.ShapeDtypeStruct((row_count, groups * HD), BF)] * 2,
        in_specs=[scalar] + [vmem] * 5,
        out_specs=[vmem] * 2,
        cost_estimate=cost(COSTS[1]),
        compiler_params=pltpu.CompilerParams(vmem_limit_bytes=8 << 20),
        name="fresh",
    )(req_scalar, hidden_in, gain, w_key, w_value, lengths)
    queries = gather_rows(query, "req")

    query_row, left, slot, local = pl.pallas_call(
        functools.partial(place_kernel, row_count, share),
        out_shape=[
            jax.ShapeDtypeStruct((blocks, 1), jnp.int32),
            jax.ShapeDtypeStruct((1, blocks), jnp.int32),
            jax.ShapeDtypeStruct((1, blocks), jnp.int32),
            jax.ShapeDtypeStruct((blocks, 1), jnp.int32),
        ],
        in_specs=[scalar, vmem, vmem],
        out_specs=[vmem] * 4,
        cost_estimate=cost(COSTS[6]),
        compiler_params=pltpu.CompilerParams(vmem_limit_bytes=8 << 20),
        name="places",
    )(req_scalar, block_slot[None, :], lengths)

    def pairs(cache):
        cache = cache.reshape(blocks, groups, HD, 2 * HD).transpose(0, 2, 1, 3)
        return cache.reshape(blocks, HD * groups, 2 * HD)

    partial = attend(
        heads, groups, CHUNK, width, query_row, left, slot, local,
        queries, pairs(k_cache), pairs(v_cache),
    )
    parts = send_rows(partial, "req")
    kv_scalar = jnp.reshape(kv_index, (1,)).astype(jnp.int32)
    token_count = row_count // kv_size
    projected = pl.pallas_call(
        functools.partial(merge_kernel, heads, groups, kv_size),
        out_shape=[jax.ShapeDtypeStruct((token_count, model), BF)] * (kv_size // 2)
        + [jax.ShapeDtypeStruct((kv_size // 2 * token_count, model), BF)],
        in_specs=[scalar] + [vmem] * (4 + sources),
        out_specs=[vmem] * (kv_size // 2 + 1),
        scratch_shapes=[pltpu.VMEM((row_count, model), F32)],
        compiler_params=pltpu.CompilerParams(vmem_limit_bytes=10 << 20),
        cost_estimate=cost(COSTS[3]),
        name="merge",
    )(kv_scalar, query, key_new, value_new, w_out, *parts)
    given = swap(projected[-1], "kv", 1)
    pieces = [projected[0]]
    for place in range(1, kv_size // 2):
        joined = given[place * token_count : (place + 1) * token_count].astype(F32)
        joined = (projected[place].astype(F32) + joined).astype(BF)
        pieces.append(swap(joined, "kv", 2 * place))
    after_attn, outgoing = pl.pallas_call(
        route_kernel,
        out_shape=[
            jax.ShapeDtypeStruct((token_count, model), F32),
            jax.ShapeDtypeStruct((token_count, model + 128), BF),
        ],
        in_specs=[scalar] + [vmem] * (5 + kv_size // 2),
        out_specs=[vmem, vmem],
        compiler_params=pltpu.CompilerParams(vmem_limit_bytes=10 << 20),
        cost_estimate=cost(COSTS[4]),
        name="route",
    )(kv_scalar, hidden_in, moe_gain.reshape(-1, 128), w_router, routes, given, *pieces)
    arrived = gather_rows(outgoing, "req")
    local_experts = w_gate_up.shape[0]
    if STAGE:
        w_gate_up = pl.pallas_call(
            stage_kernel,
            out_shape=jax.ShapeDtypeStruct(w_gate_up.shape, BF),
            in_specs=[pl.BlockSpec(memory_space=pl.ANY), far],
            out_specs=pl.BlockSpec(memory_space=pl.ANY),
            scratch_shapes=[pltpu.SemaphoreType.DMA],
            cost_estimate=cost(2.0),
            compiler_params=pltpu.CompilerParams(vmem_limit_bytes=SLIM << 20),
            name="stage",
        )(outgoing, w_gate_up)
    mixed = pl.pallas_call(
        functools.partial(expert_kernel, sources, w_router.shape[1]),
        grid=(local_experts,),
        out_shape=[jax.ShapeDtypeStruct((token_count, model), BF)] * sources,
        in_specs=[scalar]
        + [vmem] * sources
        + [
            pl.BlockSpec((1,) + w_gate_up.shape[1:], lambda i: (i, 0, 0)),
            pl.BlockSpec((1,) + w_down.shape[1:], lambda i: (i, 0, 0)),
        ],
        out_specs=[vmem] * sources,
        scratch_shapes=[
            pltpu.VMEM((sources * token_count, model + 128), BF),
            pltpu.VMEM((sources * token_count, model), F32),
        ],
        compiler_params=pltpu.CompilerParams(vmem_limit_bytes=24 << 20),
        cost_estimate=cost(COSTS[5]),
        name="experts",
    )(req_scalar, *arrived, w_gate_up, w_down)
    mixture = sum_rows(mixed, "req")
    return (after_attn + mixture).astype(BF)


def solution(mesh):
    placed = (
        P("req", None),
        P(),
        P("kv", None),
        P("kv", None),
        P("kv", None),
        P("kv", None),
        P("req", "kv", None),
        P("req", "kv", None),
        P(),
        P("req"),
        P(),
        P(),
        P("req", None, None),
        P("req", None, None),
        P(("req", "kv"), None),
    )
    return jax.shard_map(
        shards, mesh=mesh, in_specs=placed, out_specs=P(("req", "kv"), None), check_vma=False
    )
```

```python
import functools
import math

import jax
import jax.numpy as jnp
from jax import lax
from jax.experimental import pallas as pl
from jax.experimental.pallas import tpu as pltpu
from jax.sharding import PartitionSpec as P

HD = 64
FFE = 512
BLK = 128
PAGES = 3
CHUNK = 96
QLIM = 60
ALIM = 24
SLIM = 1
STAGE = True
COSTS = (12.0, 1.0, 12.0, 12.0, 12.0, 4.0, 12.0)
NEG = -1e30
BF = jnp.bfloat16
F32 = jnp.float32


def iota(shape, dim):
    return lax.broadcasted_iota(jnp.int32, shape, dim)


def swap(value, axis, distance):
    size = lax.axis_size(axis)
    return lax.ppermute(value, axis, [(source, source ^ distance) for source in range(size)])


def gather_rows(value, axis):
    size = lax.axis_size(axis)
    far = size // 2
    held = {0: value, far: swap(value, axis, far)}
    for distance in range(far - 1, 0, -1):
        held[distance] = swap(value, axis, distance)
    for distance in range(far - 1, 0, -1):
        held[far + distance] = swap(held[far], axis, distance)
    return [held[distance] for distance in range(size)]


def send_rows(values, axis):
    size = lax.axis_size(axis)
    held = {0: values[0]}
    far = size // 2
    for start in list(range(size - 2, far - 1, -2)) + list(range(2, far, 2)) + [0]:
        for distance in (start, start + 1):
            if distance:
                held[distance] = swap(values[distance], axis, distance)
    return [held[distance] for distance in sorted(held, key=lambda distance: -distance)]


def sum_rows(values, axis):
    size = lax.axis_size(axis)
    far = size // 2
    beside = [swap(values[far + distance], axis, distance) for distance in range(far - 1, 0, -1)]
    joined = values[far].astype(F32)
    for value in beside:
        joined = joined + value.astype(F32)
    joined, near = joined.astype(BF), values[1:far]
    arrived = [swap(joined, axis, far)]
    arrived += [swap(near[distance - 1], axis, distance) for distance in range(far - 1, 0, -1)]
    total = values[0].astype(F32)
    for value in arrived:
        total = total + value.astype(F32)
    return total


def cost(micros):
    return pl.CostEstimate(flops=int(micros * 1e9), bytes_accessed=int(micros * 3e6), transcendentals=0)


def project_rows(normed, weight):
    return lax.dot_general(normed, weight, (((1,), (1,)), ((), ())), preferred_element_type=F32)


def dot(left, right):
    return jnp.dot(left, right, preferred_element_type=F32)


def rotate(values, cosines, sines):
    width = values.shape[1]
    low = iota((1, 2 * HD), 1) % HD < HD // 2
    pieces = []
    for start in range(0, width, 2 * HD):
        tile = values[:, start : start + 2 * HD]
        short = 2 * HD - tile.shape[1]
        if short:
            tile = jnp.concatenate([tile, tile], 1)
        turned = jnp.where(low, pltpu.roll(tile, 2 * HD - HD // 2, 1), pltpu.roll(tile, HD // 2, 1))
        pieces.append((tile * cosines + turned * sines)[:, : 2 * HD - short])
    return pieces[0] if len(pieces) == 1 else jnp.concatenate(pieces, 1)


def tables(req_ref, length_ref, rows):
    lengths = jnp.broadcast_to(length_ref[pl.ds(req_ref[0], 1), :].astype(F32), (rows, rows))
    lengths = jnp.where(iota((rows, rows), 0) == iota((rows, rows), 1), lengths, 0.0)
    exponent = (iota((1, 2 * HD), 1) % (HD // 2)).astype(F32) * (-2.0 / HD)
    angles = jnp.sum(lengths, -1, keepdims=True) * jnp.exp(exponent * math.log(10000.0))
    sines = jnp.sin(angles)
    return jnp.cos(angles), jnp.where(iota((1, 2 * HD), 1) % HD < HD // 2, -sines, sines)


def query_kernel(req_ref, hidden_hbm, gain_hbm, weight_hbm, length_hbm, query_ref, hidden_ref, gain_ref, weight_ref,
                 length_ref, sem):
    copies = [
        pltpu.make_async_copy(source, target, sem.at[place])
        for place, (source, target) in enumerate(
            [(length_hbm, length_ref), (hidden_hbm, hidden_ref), (weight_hbm, weight_ref), (gain_hbm, gain_ref)]
        )
    ]
    for copy in copies:
        copy.start()
    for copy in copies:
        copy.wait()
    normed = rms_norm(hidden_ref[...], lanes_of(gain_ref))
    cosines, sines = tables(req_ref, length_ref, query_ref.shape[0])
    query = project_rows(normed, weight_ref[...])
    query_ref[...] = (rotate(query, cosines, sines) * 0.125).astype(BF)


def rms_norm(hidden, gain):
    hidden = hidden.astype(F32)
    scale = lax.rsqrt(jnp.mean(hidden * hidden, -1, keepdims=True) + 1e-05)
    return (hidden * scale * gain).astype(BF)


def place_kernel(rows, share, req_ref, block_ref, length_ref, query_ref, left_ref, slot_ref, local_ref):
    blocks = block_ref.shape[1]
    here = iota((blocks, blocks), 0)
    there = iota((blocks, blocks), 1)
    by_lane = block_ref[...]
    by_row = jnp.sum(jnp.where(here == there, by_lane, 0), 1, keepdims=True)
    owner = by_row // PAGES
    home = owner // rows
    local_ref[...] = owner % rows
    query_ref[...] = jnp.bitwise_xor(home, req_ref[0]) * rows + owner % rows
    lengths = lanes_of(length_ref)
    owned = owner == iota((blocks, lengths.shape[1]), 1)
    left = jnp.sum(jnp.where(owned, lengths, 0), 1, keepdims=True) - (by_row - owner * PAGES) * BLK
    left_ref[...] = jnp.sum(jnp.where(here == there, left, 0), 0, keepdims=True)
    lane_home = by_lane // PAGES // rows
    earlier = jnp.logical_and(home == lane_home, here < there)
    rank = jnp.sum(earlier.astype(jnp.int32), 0, keepdims=True)
    slot_ref[...] = jnp.bitwise_xor(lane_home, req_ref[0]) * share + rank


def lanes_of(ref):
    return jnp.concatenate([ref[row : row + 1, :] for row in range(ref.shape[0])], 1)


def fresh_kernel(req_ref, hidden_ref, gain_ref, key_weight_ref, value_weight_ref, length_ref, key_ref, value_ref):
    cosines, sines = tables(req_ref, length_ref, key_ref.shape[0])
    normed = rms_norm(hidden_ref[...], lanes_of(gain_ref))
    key = project_rows(normed, key_weight_ref[...])
    key_ref[...] = rotate(key, cosines, sines).astype(BF)
    value_ref[...] = project_rows(normed, value_weight_ref[...]).astype(BF)


def side_by_side(pairs):
    none = jnp.zeros_like(pairs[:, 0])
    first = jnp.concatenate([pairs[:, 0], none], 2)
    return jnp.concatenate([first, jnp.concatenate([none, pairs[:, 1]], 2)], 1)


def attend_kernel(heads, groups, chunk, nq, *refs):
    qrow_ref, left_ref, slot_ref, local_ref = refs[:4]
    query_refs = refs[4:4+nq]
    key_ref, value_ref = refs[4 + nq : 6 + nq]
    out_refs = refs[6 + nq : -5]
    asked_ref, laid_ref, mean_ref, level_ref, rows_ref = refs[-5:]
    blocks = qrow_ref.shape[0]
    lanes = key_ref.shape[1]
    share, width = out_refs[0].shape
    per_group = heads // groups
    feature = heads * HD
    index = pl.program_id(0)

    @pl.when(index == 0)
    def _():
        queries = jnp.concatenate([query_ref[...] for query_ref in query_refs], 0)
        picked = (iota((blocks, queries.shape[0]), 1) == qrow_ref[...]).astype(BF)
        asked_ref[...] = dot(picked, queries)
        laid_ref[...] = jnp.zeros(laid_ref.shape, F32)

    base = pl.multiple_of(index * chunk, chunk)
    rows = pl.ds(base, chunk)
    low = iota((chunk, 2 * HD), 1) < HD
    for pair in range((heads + 1) // 2):
        stop = min(feature, (pair + 1) * 2 * HD)
        tile = asked_ref[rows, pair * 2 * HD : stop]
        if tile.shape[1] < 2 * HD:
            tile = jnp.concatenate([tile, tile], 1)
        turned = pltpu.roll(tile, HD, 1)
        for odd in range(2):
            head = 2 * pair + odd
            if head < heads:
                first, second = (turned, tile) if odd else (tile, turned)
                laid_ref[pl.ds(head, chunk, 16), :] = jnp.where(low, first, 0.0)
                laid_ref[pl.ds(head + 8, chunk, 16), :] = jnp.where(low, 0.0, second)
    query = laid_ref[: chunk * 16, :].astype(BF)
    query = side_by_side(query.reshape(chunk // 2, 2, 16, 2 * HD)).reshape(chunk // 4, 64, 4 * HD)
    keys = key_ref[...].reshape(chunk // 4, 2, 2, lanes, 2 * HD)
    keys = jnp.concatenate([keys[:, :, 0], keys[:, :, 1]], 3).reshape(chunk // 4, 2 * lanes, 4 * HD)
    scores = lax.dot_general(query, keys, (((2,), (2,)), ((0,), (0,))), preferred_element_type=F32)
    scores = jnp.concatenate([scores[:, None, :32, :lanes], scores[:, None, 32:, lanes:]], 1)
    scores = scores.reshape(chunk, 16, lanes)
    cell_row = iota((8, lanes), 0)
    cell_lane = iota((8, lanes), 1)
    position = jnp.where(cell_lane % groups == cell_row // per_group, 2 * (cell_lane // groups), 1 << 20)
    position = position[None]
    remaining = [jnp.full((1, 8, lanes), left_ref[0, base + place], jnp.int32) for place in range(chunk)]
    remaining = jnp.concatenate(remaining, 0)
    usable = jnp.concatenate([position < remaining, position + 1 < remaining], 1)
    scores = jnp.where(usable, scores, NEG)
    highest = jnp.max(jnp.maximum(scores[:, :8], scores[:, 8:]), -1, keepdims=True)
    weights = jnp.where(usable, jnp.exp(scores - jnp.concatenate([highest, highest], 1)), 0.0)
    total = jnp.sum(weights[:, :8] + weights[:, 8:], -1, keepdims=True)
    weights = side_by_side(weights.astype(BF).reshape(chunk // 2, 2, 16, lanes))
    numer = lax.dot_general(weights, value_ref[...].reshape(chunk // 2, 2 * lanes, 2 * HD), (((2,), (1,)), ((0,), (0,))), preferred_element_type=F32)
    numer = numer.reshape(chunk, 16, 2 * HD)
    numer = jnp.where(iota((1, 8, 2 * HD), 2) < HD, numer[:, :8], numer[:, 8:]).reshape(chunk * 8, 2 * HD)
    numer = numer + pltpu.roll(numer, HD, 1)
    total = total.reshape(chunk * 8, 1)
    highest = highest.reshape(chunk * 8, 1)
    some = total > 0.0
    safe = jnp.where(some, total, 1.0)
    mean_ref[: chunk * 8, :] = numer / safe
    level_ref[: chunk * 8, :] = jnp.broadcast_to(jnp.where(some, highest + jnp.log(safe), NEG), (chunk * 8, 2 * HD))
    lane = iota((chunk, 2 * HD), 1)
    means = [mean_ref[pl.ds(head, chunk, 8), :] for head in range(heads)]
    extras = jnp.zeros((chunk, 2 * HD), F32)
    start = feature % (2 * HD)
    for head in range(heads):
        level = level_ref[pl.ds(head, chunk, 8), :]
        first = level.astype(BF).astype(F32)
        second = (level - first).astype(BF).astype(F32)
        third = level - first - second
        for part, piece in enumerate((first, second, third)):
            extras = jnp.where(lane == start + 4 * head + part, piece, extras)
    extras = jnp.where(lane == start + HD - 1, local_ref[...].astype(F32), extras)
    for pair in range(width // (2 * HD)):
        left = means[2 * pair] if 2 * pair < heads else extras
        right = means[2 * pair + 1] if 2 * pair + 1 < heads else extras
        rows_ref[rows, pair * 2 * HD : (pair + 1) * 2 * HD] = jnp.where(low, left, right).astype(BF)

    @pl.when(index == blocks // chunk - 1)
    def _():
        order = (slot_ref[...] == iota((blocks, blocks), 0)).astype(BF)
        sorted_rows = dot(order, rows_ref[...])
        for place, out_ref in enumerate(out_refs):
            out_ref[...] = sorted_rows[place * share : (place + 1) * share].astype(BF)

def attend(heads, groups, chunk, width, qrow, left, slot, local, queries, keys, values, limit=ALIM):
    blocks, lanes = keys.shape[:2]
    whole = pl.BlockSpec(memory_space=pltpu.VMEM)
    block = lambda *shape: pl.BlockSpec(shape, lambda i: (i,) + (0,) * (len(shape) - 1))
    return pl.pallas_call(
        functools.partial(attend_kernel, heads, groups, chunk, len(queries)),
        grid=(blocks // chunk,),
        out_shape=[jax.ShapeDtypeStruct((blocks // len(queries), width), BF)] * len(queries),
        in_specs=[whole, pl.BlockSpec(memory_space=pltpu.SMEM), whole, block(chunk, 1)] + [whole] * len(queries)
        + [block(chunk, lanes, 2 * HD)] * 2,
        out_specs=[whole] * len(queries),
        scratch_shapes=[
            pltpu.VMEM((blocks, heads * HD), F32),
            pltpu.VMEM((chunk * 16 + 16, 2 * HD), F32),
            pltpu.VMEM((chunk * 8 + 8, 2 * HD), F32),
            pltpu.VMEM((chunk * 8 + 8, 2 * HD), F32),
            pltpu.VMEM((blocks, width), BF),
        ],
        compiler_params=pltpu.CompilerParams(vmem_limit_bytes=limit << 20),
        cost_estimate=cost(COSTS[2]),
        name="attend",
    )(qrow, left, slot, local, *queries, keys, values)


def merge_kernel(heads, groups, tokens, *refs):
    kv_ref, query_ref, key_ref, value_ref, weight_ref = refs[:5]
    keep_refs = refs[-2 - tokens // 2 : -2]
    give_ref, result_ref = refs[-2:]
    part_refs = refs[5 : -2 - tokens // 2]
    parts = jnp.concatenate([part_ref[...] for part_ref in part_refs], 0)
    rows = query_ref.shape[0]
    blocks, width = parts.shape
    per_group = heads // groups
    feature = heads * HD
    row = iota((32, width), 0)
    column = iota((32, width), 1) - feature
    wanted = jnp.where(row < 24, (row % 8) * 4 + row // 8, HD - 1)
    pick = jnp.logical_and(column == wanted, jnp.logical_or(row == 24, row % 8 < heads))
    pick = jnp.logical_and(pick, row <= 24).astype(BF)
    extras = lax.dot_general(pick, parts, (((1,), (1,)), ((), ())), preferred_element_type=F32)
    levels = extras[0:8] + extras[8:16] + extras[16:24]
    local = extras[24:25].astype(jnp.int32)
    member = local == iota((rows, blocks), 0)

    source = iota((groups * HD, width), 0)
    target = iota((groups * HD, width), 1)
    same = jnp.logical_and(source // HD == target // (HD * per_group), source % HD == target % HD)
    widen = same.astype(BF)
    key = dot(key_ref[...], widen)
    value = dot(value_ref[...], widen)
    products = query_ref[...].astype(F32) * key[:, :feature]
    lane_head = iota((rows, width), 1) // HD
    shares, owns, totals = [], [], []
    for head in range(heads):
        own = jnp.sum(jnp.where(lane_head[:, :feature] == head, products, 0.0), -1, keepdims=True)
        level = levels[head : head + 1]
        highest = jnp.max(jnp.where(member, level, NEG), -1, keepdims=True)
        highest = jnp.maximum(highest, own)
        weights = jnp.where(member, jnp.exp(level - highest), 0.0).astype(BF)
        own_weight = jnp.exp(own - highest)
        shares.append(weights)
        owns.append(own_weight)
        totals.append(jnp.sum(weights.astype(F32), -1, keepdims=True) + own_weight)
    numers = dot(jnp.concatenate(shares, 0), parts)
    joined = jnp.zeros((rows, width), F32)
    for head in range(heads):
        numer = numers[head * rows : (head + 1) * rows] + owns[head] * value
        joined = jnp.where(lane_head == head, numer / totals[head], joined)
    attended = joined[:, :feature].astype(BF)
    result_ref[...] = dot(attended, weight_ref[...])
    count = rows // tokens
    for place in range(tokens):
        start = pl.multiple_of(jnp.bitwise_xor(kv_ref[0], place) * count, count)
        piece = result_ref[pl.ds(start, count), :].astype(BF)
        if place % 2:
            give_ref[place // 2 * count : (place // 2 + 1) * count, :] = piece
        else:
            keep_refs[place // 2][...] = piece


def route_kernel(kv_ref, hidden_ref, gain_ref, router_ref, routes_ref, given_ref, *refs):
    piece_refs = refs[:-2]
    after_ref, out_ref = refs[-2:]
    count, model = after_ref.shape
    start = pl.multiple_of(kv_ref[0] * count, count)
    total = given_ref[:count, :].astype(F32)
    for piece_ref in piece_refs:
        total = total + piece_ref[...].astype(F32)
    after = hidden_ref[pl.ds(start, count), :].astype(F32) + total
    after_ref[...] = after
    scale = lax.rsqrt(jnp.mean(after * after, -1, keepdims=True) + 1e-05)
    normed = (after * scale * lanes_of(gain_ref)).astype(BF)
    out_ref[:, :model] = normed
    experts = router_ref.shape[1]
    logits = dot(normed, router_ref[...])
    expert = iota((count, experts), 1)
    chosen = expert == routes_ref[:, 0:1]
    for turn in range(1, routes_ref.shape[1]):
        chosen = jnp.logical_or(chosen, expert == routes_ref[:, turn : turn + 1])
    logits = jnp.where(chosen, logits, NEG)
    gates = jnp.where(chosen, jnp.exp(logits - jnp.max(logits, -1, keepdims=True)), 0.0)
    gates = gates / jnp.sum(gates, -1, keepdims=True)
    high = gates.astype(BF).astype(F32)
    spare = jnp.zeros((count, 128 - 2 * experts), F32)
    out_ref[:, model:] = jnp.concatenate([high, gates - high, spare], 1).astype(BF)


def stage_kernel(order_ref, source_ref, target_ref, sem):
    copy = pltpu.make_async_copy(source_ref, target_ref, sem)
    copy.start()
    copy.wait()


def expert_kernel(sources, experts, req_ref, *refs):
    token_refs = refs[:sources]
    up_ref, down_ref = refs[sources : sources + 2]
    out_refs = refs[sources + 2 : -2]
    tokens_ref, mixed_ref = refs[-2:]
    index = pl.program_id(0)
    count, model = out_refs[0].shape
    hidden = down_ref.shape[1]

    @pl.when(index == 0)
    def _():
        for place, token_ref in enumerate(token_refs):
            tokens_ref[place * count : (place + 1) * count, :] = token_ref[...]

    lane = iota((sources * count, 128), 1)
    mine = req_ref[0] * pl.num_programs(0) + index
    gates = tokens_ref[:, model:].astype(F32)
    picked = jnp.logical_or(lane == mine, lane == mine + experts)
    gate = jnp.sum(jnp.where(picked, gates, 0.0), -1, keepdims=True)
    both = dot(tokens_ref[:, :model], up_ref[0])
    active = (jax.nn.silu(both[:, :hidden]) * both[:, hidden:]).astype(BF)
    produced = dot(active, down_ref[0]).astype(BF).astype(F32) * gate

    @pl.when(index == 0)
    def _():
        mixed_ref[...] = produced

    @pl.when(index > 0)
    def _():
        mixed_ref[...] += produced

    @pl.when(index == pl.num_programs(0) - 1)
    def _():
        for place, out_ref in enumerate(out_refs):
            out_ref[...] = mixed_ref[place * count : (place + 1) * count, :].astype(BF)


def shards(
    hidden_in,
    attn_gain,
    w_query,
    w_key,
    w_value,
    w_out,
    k_cache,
    v_cache,
    cache_len,
    block_slot,
    moe_gain,
    w_router,
    w_gate_up,
    w_down,
    routes,
):
    req_index = lax.axis_index("req")
    kv_index = lax.axis_index("kv")
    sources = lax.axis_size("req")
    kv_size = lax.axis_size("kv")
    row_count, model = hidden_in.shape
    heads = w_query.shape[0] // HD
    groups = w_key.shape[0] // HD
    blocks = k_cache.shape[0]
    requests = cache_len.shape[0]
    share = blocks // sources
    width = -(-(heads * HD + HD) // 128) * 128

    vmem = pl.BlockSpec(memory_space=pltpu.VMEM)
    scalar = pl.BlockSpec(memory_space=pltpu.SMEM)
    req_scalar = jnp.reshape(req_index, (1,)).astype(jnp.int32)
    far = pl.BlockSpec(memory_space=pltpu.HBM)
    gain = attn_gain.reshape(-1, 128)
    lengths = cache_len.reshape(sources, row_count)
    query = pl.pallas_call(
        query_kernel,
        out_shape=jax.ShapeDtypeStruct((row_count, heads * HD), BF),
        in_specs=[scalar] + [far] * 4,
        out_specs=vmem,
        scratch_shapes=[
            pltpu.VMEM((row_count, model), BF),
            pltpu.VMEM((model // 128, 128), F32),
            pltpu.VMEM(w_query.shape, BF),
            pltpu.VMEM((sources, row_count), jnp.int32),
            pltpu.SemaphoreType.DMA((4,)),
        ],
        cost_estimate=cost(COSTS[0]),
        compiler_params=pltpu.CompilerParams(vmem_limit_bytes=QLIM << 20),
        name="query",
    )(req_scalar, hidden_in, gain, w_query, lengths)
    key_new, value_new = pl.pallas_call(
        fresh_kernel,
        out_shape=[jax.ShapeDtypeStruct((row_count, groups * HD), BF)] * 2,
        in_specs=[scalar] + [vmem] * 5,
        out_specs=[vmem] * 2,
        cost_estimate=cost(COSTS[1]),
        compiler_params=pltpu.CompilerParams(vmem_limit_bytes=8 << 20),
        name="fresh",
    )(req_scalar, hidden_in, gain, w_key, w_value, lengths)
    queries = gather_rows(query, "req")

    query_row, left, slot, local = pl.pallas_call(
        functools.partial(place_kernel, row_count, share),
        out_shape=[
            jax.ShapeDtypeStruct((blocks, 1), jnp.int32),
            jax.ShapeDtypeStruct((1, blocks), jnp.int32),
            jax.ShapeDtypeStruct((1, blocks), jnp.int32),
            jax.ShapeDtypeStruct((blocks, 1), jnp.int32),
        ],
        in_specs=[scalar, vmem, vmem],
        out_specs=[vmem] * 4,
        cost_estimate=cost(COSTS[6]),
        compiler_params=pltpu.CompilerParams(vmem_limit_bytes=8 << 20),
        name="places",
    )(req_scalar, block_slot[None, :], lengths)

    def pairs(cache):
        cache = cache.reshape(blocks, groups, HD, 2 * HD).transpose(0, 2, 1, 3)
        return cache.reshape(blocks, HD * groups, 2 * HD)

    partial = attend(
        heads, groups, CHUNK, width, query_row, left, slot, local,
        queries, pairs(k_cache), pairs(v_cache),
    )
    parts = send_rows(partial, "req")
    kv_scalar = jnp.reshape(kv_index, (1,)).astype(jnp.int32)
    token_count = row_count // kv_size
    projected = pl.pallas_call(
        functools.partial(merge_kernel, heads, groups, kv_size),
        out_shape=[jax.ShapeDtypeStruct((token_count, model), BF)] * (kv_size // 2)
        + [jax.ShapeDtypeStruct((kv_size // 2 * token_count, model), BF)],
        in_specs=[scalar] + [vmem] * (4 + sources),
        out_specs=[vmem] * (kv_size // 2 + 1),
        scratch_shapes=[pltpu.VMEM((row_count, model), F32)],
        compiler_params=pltpu.CompilerParams(vmem_limit_bytes=10 << 20),
        cost_estimate=cost(COSTS[3]),
        name="merge",
    )(kv_scalar, query, key_new, value_new, w_out, *parts)
    given = swap(projected[-1], "kv", 1)
    pieces = [projected[0]]
    for place in range(1, kv_size // 2):
        joined = given[place * token_count : (place + 1) * token_count].astype(F32)
        joined = (projected[place].astype(F32) + joined).astype(BF)
        pieces.append(swap(joined, "kv", 2 * place))
    after_attn, outgoing = pl.pallas_call(
        route_kernel,
        out_shape=[
            jax.ShapeDtypeStruct((token_count, model), F32),
            jax.ShapeDtypeStruct((token_count, model + 128), BF),
        ],
        in_specs=[scalar] + [vmem] * (5 + kv_size // 2),
        out_specs=[vmem, vmem],
        compiler_params=pltpu.CompilerParams(vmem_limit_bytes=10 << 20),
        cost_estimate=cost(COSTS[4]),
        name="route",
    )(kv_scalar, hidden_in, moe_gain.reshape(-1, 128), w_router, routes, given, *pieces)
    arrived = gather_rows(outgoing, "req")
    local_experts = w_gate_up.shape[0]
    if STAGE:
        w_gate_up = pl.pallas_call(
            stage_kernel,
            out_shape=jax.ShapeDtypeStruct(w_gate_up.shape, BF),
            in_specs=[pl.BlockSpec(memory_space=pl.ANY), far],
            out_specs=pl.BlockSpec(memory_space=pl.ANY),
            scratch_shapes=[pltpu.SemaphoreType.DMA],
            cost_estimate=cost(2.0),
            compiler_params=pltpu.CompilerParams(vmem_limit_bytes=SLIM << 20),
            name="stage",
        )(outgoing, w_gate_up)
    mixed = pl.pallas_call(
        functools.partial(expert_kernel, sources, w_router.shape[1]),
        grid=(local_experts,),
        out_shape=[jax.ShapeDtypeStruct((token_count, model), BF)] * sources,
        in_specs=[scalar]
        + [vmem] * sources
        + [
            pl.BlockSpec((1,) + w_gate_up.shape[1:], lambda i: (i, 0, 0)),
            pl.BlockSpec((1,) + w_down.shape[1:], lambda i: (i, 0, 0)),
        ],
        out_specs=[vmem] * sources,
        scratch_shapes=[
            pltpu.VMEM((sources * token_count, model + 128), BF),
            pltpu.VMEM((sources * token_count, model), F32),
        ],
        compiler_params=pltpu.CompilerParams(vmem_limit_bytes=24 << 20),
        cost_estimate=cost(COSTS[5]),
        name="experts",
    )(req_scalar, *arrived, w_gate_up, w_down)
    mixture = sum_rows(mixed, "req")
    return (after_attn + mixture).astype(BF)


def solution(mesh):
    placed = (
        P("req", None),
        P(),
        P("kv", None),
        P("kv", None),
        P("kv", None),
        P("kv", None),
        P("req", "kv", None),
        P("req", "kv", None),
        P(),
        P("req"),
        P(),
        P(),
        P("req", None, None),
        P("req", None, None),
        P(("req", "kv"), None),
    )
    return jax.shard_map(
        shards, mesh=mesh, in_specs=placed, out_specs=P(("req", "kv"), None), check_vma=False
    )
```
